256 devices in a mesh: expert: 32 (over x, z), half: 2 (over core), dp: 4 (over y).
Axes of the slice: x: 4, y: 4, z: 8, core: 2. Of those that a mesh axis runs over, the one named last changes fastest.
Arguments:
- tokens_in: bfloat16 [128, 2, 12, 3584], P(('expert', 'dp')), may hold values from -6 to 6
- cotangent: bfloat16 [128, 2, 12, 3584], P(('expert', 'dp')), may hold values from -1.5 to 1.5
- expert_ids: int32 [128, 2, 12, 8], P(('expert', 'dp')), may hold values from 0 to 31, all different within a row; in each aligned block of 12 rows (0 to 11, 12 to 23, ..., all dimensions but the last counted through in order) at most 6 rows name the same one
- gate_probs: bfloat16 [128, 2, 12, 8], P(('expert', 'dp')), may hold values from 0.049804688 to 0.5
- gate_weight: bfloat16 [32, 3584, 1024], P('expert', 'dp', 'half'), may hold values from -0.09375 to 0.09375
- up_weight: bfloat16 [32, 3584, 1024], P('expert', 'dp', 'half'), may hold values from -0.09375 to 0.09375
- down_weight: bfloat16 [32, 3584, 1024], P('expert', 'dp', 'half'), may hold values from -0.1875 to 0.1875
Outputs:
- token_grad: bfloat16 [128, 2, 12, 3584], P(('expert', 'dp'), 'half')
- route_grad: bfloat16 [128, 2, 12, 8], P(('expert', 'dp'), 'half')
- gate_weight_grad: bfloat16 [32, 3584, 1024], P('expert', 'dp', 'half')
- up_weight_grad: bfloat16 [32, 3584, 1024], P('expert', 'dp', 'half')
- down_weight_grad: bfloat16 [32, 3584, 1024], P('expert', 'dp', 'half')
The draws below stay inside these ranges and needn't reach their ends.
Inputs may be any that keep to these rules, and one draw needn't show every extreme that they name: `expert_ids`: each row names 8 different experts. Among the 12 tokens of one owner block (the aligned blocks of the last two leading dimensions), no expert is named by more than 6 tokens, and in every draw some expert is named by exactly 6 tokens of some block.
All inputs are finite; a program needn't handle non-finite values.
Results may differ from the reference program's by a relative error of at most 0.017.
Values may be sent and summed in bfloat16 or wider, within the bound.
A program may use at most 192 MiB of HBM per device.

```python
import math
import jax
import jax.numpy as jnp
import numpy as np
from jax import lax

D = 3584
FF = 1024
TOP = 8
EXPERTS = 32
HALF_TOK = 12
MOST = 6
GROUPS = 128
N_EXPERT = 32
N_DP = 4


def shard_levels(rng, extent, shards, least, largest):
    factor_of = 1.0
    for position, shards_of in shards:
        heights = jax.random.uniform(jax.random.fold_in(jax.random.fold_in(rng, 6), position), (shards_of,), jnp.float32, least / len(shards), largest / len(shards))
        factor_of = factor_of * jnp.repeat(jnp.exp(heights), extent[position] // shards_of).reshape((-1,) + (1,) * (len(extent) - 1 - position))
    return factor_of


def shared_out(own_key, own, number, rows, amount, top, reach, slope):
    sequence = jax.random.permutation(own_key, amount)
    packed, ordinary = shares(amount, rows * top, reach, slope, True), shares(amount, rows * top, reach, slope, False)
    places = jnp.arange(amount)

    def named(lengths, offset_by):
        used = int((lengths > 0).sum())
        fixed = max(1, used // 4)
        shifted = fixed + (places - fixed + offset_by * (used - fixed)) % max(1, amount - fixed)
        return jnp.zeros((amount,), jnp.int32).at[sequence[jnp.where(places < fixed, places, shifted)]].set(jnp.asarray(lengths, jnp.int32))

    lengths = jnp.where(number % 4 == 0, named(packed, number // 4), named(ordinary, number - number // 4 - 1))
    mixed = jax.random.permutation(jax.random.fold_in(own, 3), amount)
    source_of, sink = mixed[0:amount // 2 * 2:2], mixed[1:amount // 2 * 2:2]
    room = jnp.minimum(lengths[source_of] - 1, reach - lengths[sink]) // 2
    room = jnp.where((source_of == sequence[0]) | (sink == sequence[0]) | (lengths[sink] == 0), 0, jnp.maximum(room, 0))
    shifted = jax.random.randint(jax.random.fold_in(own, 4), (amount // 2,), 0, 1 << 20) % (room + 1)
    lengths = lengths.at[source_of].add(-shifted).at[sink].add(shifted)
    members = jnp.searchsorted(jnp.cumsum(lengths), jnp.arange(rows * top), side="right").astype(jnp.int32)
    grid = members.reshape(top, rows).T
    grid = grid[jax.random.permutation(jax.random.fold_in(own, 1), rows)]
    offset_by = jax.random.randint(jax.random.fold_in(own, 2), (rows, 1), 0, top)
    return jnp.take_along_axis(grid, (jnp.arange(top)[None, :] + offset_by) % top, axis=1)


def shares(count, total, bound, slope, full):
    weights = [(1 << 20) // math.isqrt(rank ** slope) + 1 for rank in range(1, count + 1)]
    largest = bound if full else min(bound, max(-(-total // count), total * weights[0] // sum(weights)))
    least = 1 if total - largest >= count - 1 else 0
    holding, surplus = [largest] + [least] * (count - 1), total - largest - least * (count - 1)
    while surplus > 0:
        candidates = [i for i in range(1, count) if holding[i] < largest] or [i for i in range(1, count) if holding[i] < bound]
        whole, left = sum([weights[i] for i in candidates]), surplus
        for i in candidates:
            addition = min(bound - holding[i], max(1, left * weights[i] // whole), surplus)
            holding[i] = holding[i] + addition
            surplus = surplus - addition
    return np.array(holding)


def bell_draw(rng, dims, scale, limit, pieces=(), kind=jnp.bfloat16):
    factor_of = shard_levels(rng, dims, pieces, -0.22, 0.18) if pieces else 1.0
    drawn = jax.random.normal(rng, dims, jnp.float32) * scale * factor_of
    return jnp.minimum(jnp.maximum(drawn, -limit), limit).astype(kind)


def setup_inputs(seed: int = 0) -> dict:
    key_of = jax.random.split(jax.random.key(seed), 8)
    tokens_in = bell_draw(key_of[0], (GROUPS, 2, HALF_TOK, D), 1.0, 6.0, ((0, 128),))
    cotangent = bell_draw(key_of[1], (GROUPS, 2, HALF_TOK, D), 0.25, 1.5, ((0, 128),))
    expert_ids_keys = jax.random.split(jax.random.fold_in(key_of[2], 1), GROUPS * 2 * HALF_TOK // HALF_TOK)
    expert_ids_turns = jax.random.permutation(jax.random.fold_in(key_of[2], 3), GROUPS * 2 * HALF_TOK // HALF_TOK)
    expert_ids = jax.vmap(lambda own, number: shared_out(jax.random.fold_in(key_of[2], 2), own, number, HALF_TOK, EXPERTS, TOP, MOST, 2))(expert_ids_keys, expert_ids_turns).reshape((GROUPS, 2, HALF_TOK, TOP))
    gate_probs = jnp.clip(0.049804688 + 0.4501953 * jax.random.uniform(key_of[3], (GROUPS, 2, HALF_TOK, TOP), jnp.float32) ** shard_levels(key_of[3], (GROUPS, 2, HALF_TOK, TOP), ((0, 128),), -0.2, 0.2), 0.049804688, 0.5).astype(jnp.bfloat16)
    gate_weight = bell_draw(key_of[4], (EXPERTS, D, FF), D ** -0.5, 0.09375, ((0, 32), (1, 4), (2, 2)))
    up_weight = bell_draw(key_of[5], (EXPERTS, D, FF), D ** -0.5, 0.09375, ((0, 32), (1, 4), (2, 2)))
    down_weight = bell_draw(key_of[6], (EXPERTS, D, FF), FF ** -0.5, 0.1875, ((0, 32), (1, 4), (2, 2)))
    return dict(tokens_in=tokens_in, cotangent=cotangent, expert_ids=expert_ids, gate_probs=gate_probs, gate_weight=gate_weight, up_weight=up_weight, down_weight=down_weight)


def route_slots(route_ids, route_gates, first_expert, expert_count):
    experts_here = first_expert + jnp.arange(expert_count, dtype=jnp.int32)
    matched = route_ids[..., None, :, :] == experts_here[:, None, None]
    chosen = jnp.any(matched, axis=-1)
    slot_rank = jnp.cumsum(chosen.astype(jnp.int32), axis=-1) - 1
    slot_ids = jnp.arange(MOST, dtype=jnp.int32)
    slot_pick = jnp.logical_and(chosen[..., None, :], slot_rank[..., None, :] == slot_ids[:, None])
    route_gate = jnp.sum(jnp.where(matched, route_gates.astype(jnp.float32)[..., None, :, :], 0.0), axis=-1)
    slot_gate = jnp.sum(jnp.where(slot_pick, route_gate[..., None, :], 0.0), axis=-1)
    return slot_pick, matched, slot_gate


def silu_parts(pre_act):
    sigma = jax.nn.sigmoid(pre_act)
    return pre_act * sigma, sigma * (1.0 + pre_act * (1.0 - sigma))


def rounded_term(left, right):
    term = jnp.einsum("aprd,aprh->pdh", left, right)
    return lax.optimization_barrier(term.astype(jnp.bfloat16)).astype(jnp.float32)


def reference(tokens_in, cotangent, expert_ids, gate_probs, gate_weight, up_weight, down_weight):
    groups, halves, half_tok, model_width = tokens_in.shape
    x_all = tokens_in.astype(jnp.float32)
    dy_all = cotangent.astype(jnp.float32)
    slot_rows = groups * halves * MOST

    def micro(values):
        return values.reshape(N_EXPERT, N_DP, halves * MOST, -1).astype(jnp.float32)

    def per_expert(running, inputs):
        token_acc, route_acc = running
        expert, gate_w, up_w, down_w = inputs
        slot_pick, matched, slot_gate = route_slots(expert_ids, gate_probs, expert, 1)
        pick_f = slot_pick[:, :, 0].astype(jnp.float32)
        matched = matched[:, :, 0]
        slot_x = jnp.einsum("ghst,ghtd->ghsd", pick_f, x_all).astype(jnp.bfloat16)
        slot_dy = jnp.einsum("ghst,ghtd->ghsd", pick_f, dy_all).astype(jnp.bfloat16)
        flat_x = slot_x.reshape(slot_rows, model_width)
        flat_dy = slot_dy.reshape(slot_rows, model_width)
        gate_col = slot_gate[:, :, 0].reshape(slot_rows, 1)
        gate_act = jnp.dot(flat_x, gate_w, preferred_element_type=jnp.float32)
        up_act = jnp.dot(flat_x, up_w, preferred_element_type=jnp.float32)
        back_act = jnp.dot(flat_dy, down_w, preferred_element_type=jnp.float32)
        active, silu_slope = silu_parts(gate_act)
        hidden = (active * up_act).astype(jnp.bfloat16)
        grad_gate = (gate_col * back_act * up_act * silu_slope).astype(jnp.bfloat16)
        grad_up = (gate_col * back_act * active).astype(jnp.bfloat16)
        scaled = (gate_col * flat_dy.astype(jnp.float32)).astype(jnp.bfloat16)
        row_grad = (jnp.dot(grad_gate, gate_w.T, preferred_element_type=jnp.float32)
                    + jnp.dot(grad_up, up_w.T, preferred_element_type=jnp.float32)).astype(jnp.bfloat16)
        row_route = jnp.sum(back_act * hidden.astype(jnp.float32), axis=1).astype(jnp.bfloat16)
        token_acc = token_acc + jnp.einsum("ghst,ghsd->ghtd", pick_f, row_grad.reshape(groups, halves, MOST, model_width).astype(jnp.float32))
        per_token = jnp.einsum("ghst,ghs->ght", pick_f, row_route.reshape(groups, halves, MOST).astype(jnp.float32))
        route_acc = route_acc + jnp.where(matched, per_token[..., None], 0.0)
        gate_grad = jnp.sum(rounded_term(micro(flat_x), micro(grad_gate)), axis=0).astype(jnp.bfloat16)
        up_grad = jnp.sum(rounded_term(micro(flat_x), micro(grad_up)), axis=0).astype(jnp.bfloat16)
        down_grad = jnp.sum(rounded_term(micro(scaled), micro(hidden)), axis=0).astype(jnp.bfloat16)
        return (token_acc, route_acc), (gate_grad, up_grad, down_grad)

    start_acc = (jnp.zeros(tokens_in.shape, jnp.float32), jnp.zeros(expert_ids.shape, jnp.float32))
    expert_list = jnp.arange(EXPERTS, dtype=jnp.int32)
    finals, weight_grads = lax.scan(per_expert, start_acc, (expert_list, gate_weight, up_weight, down_weight))
    token_acc, route_acc = finals
    return (token_acc.astype(jnp.bfloat16), route_acc.astype(jnp.bfloat16),
            weight_grads[0], weight_grads[1], weight_grads[2])
```

```python
import functools

import jax
import jax.numpy as jnp
import numpy as np
from jax import lax
from jax.experimental import pallas as pl
from jax.experimental.pallas import tpu as pltpu
from jax.sharding import PartitionSpec as P

MESH = pl.DeviceIdType.MESH
BF16 = jnp.bfloat16
F32 = jnp.float32

MOST = 6
TOK = 12
PAD = 16
NX, NY, NZ = 4, 4, 8
RING = NX * NZ
LAST = RING // 2
SPAN = 4
CHUNKS = RING // SPAN
UNIT_TOK = NY * TOK
UNIT = NY * MOST
TOKENS = 2 * SPAN * UNIT_TOK
SLOTS = 2 * SPAN * UNIT
PART = SLOTS // NY
LANES = 128


def rem(a, b):
    return lax.rem(a, jnp.int32(b))


def div(a, b):
    return lax.div(a, jnp.int32(b))


def ring_position(expert, half):
    x, z = div(expert, NZ), rem(expert, NZ)
    first = 4 * z + rem(x + z, 4)
    turn = rem(z + 5 * x, NZ)
    second = 4 * x + 16 * div(turn, 4) + rem(turn, 4)
    return first + half * (second - first)


def ring_expert(position, half):
    group, inner = div(position, 4), rem(position, 4)
    first = rem(inner + 3 * group, NX) * NZ + group
    second = rem(group, NX) * NZ + rem(3 * group + inner, NZ)
    return first + half * (second - first)


def matmul(a, b, a_dim=1, b_dim=0):
    return lax.dot_general(a, b, (((a_dim,), (b_dim,)), ((), ())), preferred_element_type=F32)


def kernel(
    width,
    hidden,
    stage,
    w_gate,
    w_up,
    w_down,
    ids,
    before_chunk,
    slot_base,
    squeeze,
    before_own,
    spread,
    gather,
    slot_of,
    same_part,
    token_out,
    route_out,
    gate_out,
    up_out,
    down_out,
    own,
    unit_x,
    unit_d,
    slot_x,
    slot_s,
    gates,
    part,
    sum_one,
    sum_two,
    act,
    row_part,
    row_other,
    row_send,
    row_back,
    fin_send,
    fin_recv,
    acc,
    own_sem,
    ring_sem,
    twin_sem,
    sum_sem,
    act_sem,
    half_sem,
    back_send,
    back_recv,
    fin_sem,
):
    expert, half, dp = lax.axis_index("expert"), lax.axis_index("half"), lax.axis_index("dp")
    other = 1 - half
    position = ring_position(expert, half)
    ahead = ring_expert(rem(position + 1, RING), half)
    behind = ring_expert(rem(position + RING - 1, RING), half)
    y_next, y_last, y_far = rem(dp + 1, NY), rem(dp + 3, NY), rem(dp + 2, NY)
    three = 3 * hidden
    mid = three // 2

    def remote(src, dst, send, recv, where):
        return pltpu.make_async_remote_copy(
            src_ref=src, dst_ref=dst, send_sem=send, recv_sem=recv, device_id=where, device_id_type=MESH
        )

    barrier = pltpu.get_barrier_semaphore()

    def greet(i, carry):
        pl.semaphore_signal(
            barrier, inc=1, device_id={"expert": rem(expert + i, RING)}, device_id_type=MESH
        )
        return carry

    lax.fori_loop(1, RING, greet, 0)
    for r in range(1, NY):
        pl.semaphore_signal(barrier, inc=1, device_id={"dp": rem(dp + r, NY)}, device_id_type=MESH)
    pl.semaphore_signal(barrier, inc=1, device_id={"half": other}, device_id_type=MESH)
    pl.semaphore_wait(barrier, RING - 1 + NY - 1 + 1)

    def own_copy(r):
        return remote(
            stage.at[rem(dp + r, NY)],
            own.at[dp],
            own_sem.at[0, r],
            own_sem.at[1, r],
            {"dp": rem(dp + r, NY)},
        )

    def own_arrival(r):
        source = rem(dp + NY - r, NY)
        return remote(stage.at[source], own.at[source], own_sem.at[0, r], own_sem.at[1, r], {"dp": source})

    for r in range(1, NY):
        own_copy(r).start()
    own[dp] = stage[dp]
    acc[...] = jnp.zeros_like(acc)
    for r in range(1, NY):
        own_arrival(r).wait_recv()
    own_rows = own[...].reshape(NY * PAD, 2 * width + LANES)
    packed = matmul(squeeze[...], own_rows).astype(BF16)
    unit_x[half, 0] = packed[:, : width + LANES]
    unit_d[half, 0] = packed[:, width + LANES :]

    def ring_x(step, toward, src, dst):
        way = 0 if toward is ahead else 1
        return remote(
            unit_x.at[half, src],
            unit_x.at[half, dst],
            ring_sem.at[0, 0, way, step - 1],
            ring_sem.at[0, 1, way, step - 1],
            {"expert": toward},
        )

    def ring_d(step, toward, src, dst):
        way = 0 if toward is ahead else 1
        return remote(
            unit_d.at[half, src],
            unit_d.at[half, dst],
            ring_sem.at[1, 0, way, step - 1],
            ring_sem.at[1, 1, way, step - 1],
            {"expert": toward},
        )

    ring_x(1, ahead, 0, 2).start()
    ring_x(1, behind, 0, 1).start()
    ring_d(1, ahead, 0, 2).start()
    ring_d(1, behind, 0, 1).start()

    def ring_step(step):
        fore, aft = 2 * step - 1, 2 * step
        more, inner = step + 1 < LAST, step < LAST
        ring_x(step, behind, fore, fore).wait_recv()

        @pl.when(inner)
        def _():
            ring_x(step + 1, behind, fore, fore + 2).start()
            ring_d(step, behind, fore, fore).wait_recv()
            ring_x(step, ahead, aft, aft).wait_recv()

        @pl.when(more)
        def _():
            ring_d(step + 1, behind, fore, fore + 2).start()
            ring_x(step + 1, ahead, aft, aft + 2).start()

        @pl.when(inner)
        def _():
            ring_d(step, ahead, aft, aft).wait_recv()

        @pl.when(more)
        def _():
            ring_d(step + 1, ahead, aft, aft + 2).start()

        @pl.when(step == LAST - 1)
        def _():
            ring_d(step + 1, ahead, aft, fore + 2).start()

        @pl.when(step == LAST)
        def _():
            ring_d(step, ahead, fore, fore).wait_recv()

    def twin_x(c, block):
        span = pl.ds(c * SPAN, SPAN)
        return remote(
            unit_x.at[block, span],
            unit_x.at[block, span],
            twin_sem.at[0, 0, c],
            twin_sem.at[0, 1, c],
            {"half": other},
        )

    def twin_d(c, block):
        span = pl.ds(c * SPAN, SPAN)
        return remote(
            unit_d.at[block, span],
            unit_d.at[block, span],
            twin_sem.at[1, 0, c],
            twin_sem.at[1, 1, c],
            {"half": other},
        )

    def give_twin(c):
        twin_x(c, half).start()
        twin_d(c, half).start()

    def sum_copy(stage_no, c, way, src, dst):
        return remote(
            src,
            dst,
            sum_sem.at[stage_no, 0, way, c],
            sum_sem.at[stage_no, 1, way, c],
            {"dp": y_next if way == 0 else y_last},
        )

    def act_copy(stage_no, c, way, view):
        return remote(
            view,
            view,
            act_sem.at[stage_no, 0, way, c],
            act_sem.at[stage_no, 1, way, c],
            {"dp": y_next if way == 0 else y_last},
        )

    def columns(way):
        return pl.ds(way * mid, mid)

    def first_sum(c, way):
        return sum_copy(0, c, way, part.at[c, y_far, :, columns(way)], sum_one.at[c, way])

    def second_sum(c, way):
        toward = y_next if way == 0 else y_last
        return sum_copy(1, c, way, part.at[c, toward], sum_two.at[c, way])

    def select(c):
        twin_x(c, other).wait_recv()
        twin_d(c, other).wait_recv()
        span = pl.ds(c * SPAN, SPAN)
        block_x = [unit_x[b, span].reshape(SPAN * UNIT_TOK, width + LANES) for b in range(2)]
        all_x = jnp.concatenate(block_x, axis=0)
        is_expert = lax.broadcasted_iota(jnp.int32, (8, LANES), 1) == expert
        gate_row = matmul(is_expert.astype(BF16), all_x[:, width:], 1, 1)
        chosen = gate_row > 0.0
        rank = matmul(chosen.astype(BF16), before_chunk[...])
        place = jnp.where(chosen, slot_base[...] + rank, -1.0).astype(jnp.int32)
        row = lax.broadcasted_iota(jnp.int32, (SLOTS, TOKENS), 0)
        pick = (row == place[:1]).astype(BF16)
        gate_wide = matmul(
            pick, jnp.broadcast_to(gate_row[:1], (LANES, TOKENS)).astype(BF16), 1, 1
        )
        gates[c] = gate_wide
        slots = matmul(pick, all_x[:, :width]).astype(BF16)
        slot_x[c] = slots
        block_d = [unit_d[b, span].reshape(SPAN * UNIT_TOK, width) for b in range(2)]
        slots_d = matmul(pick, jnp.concatenate(block_d, axis=0))
        slot_s[c] = (gate_wide[:, :1] * slots_d).astype(BF16)
        shape = (NY, PART, hidden)
        part[c, :, :, 0:hidden] = matmul(slots, w_gate[...]).astype(BF16).reshape(shape)
        part[c, :, :, hidden : 2 * hidden] = matmul(slots, w_up[...]).astype(BF16).reshape(shape)
        part[c, :, :, 2 * hidden :] = (
            matmul(slots_d.astype(BF16), w_down[...]).astype(BF16).reshape(shape)
        )
        for way in range(2):
            first_sum(c, way).start()

    def add_passing(c):
        for way in range(2):
            first_sum(c, way).wait_recv()
            toward = y_next if way == 0 else y_last
            here = part[c, toward, :, columns(way)].astype(F32)
            part[c, toward, :, columns(way)] = (here + sum_one[c, way].astype(F32)).astype(BF16)
            second_sum(c, way).start()

    def activate(c):
        for way in range(2):
            second_sum(c, way).wait_recv()
        summed = (
            part[c, dp].astype(F32) + sum_two[c, 0].astype(F32) + sum_two[c, 1].astype(F32)
        )
        gate_act, up_act, back = (
            summed[:, :hidden],
            summed[:, hidden : 2 * hidden],
            summed[:, 2 * hidden :],
        )
        gate_col = gates[c, pl.ds(pl.multiple_of(dp * PART, PART), PART), :][:, :1]
        sigma = jax.nn.sigmoid(gate_act)
        active = gate_act * sigma
        slope = sigma * (1.0 + gate_act * (1.0 - sigma))
        units = (active * up_act).astype(BF16)
        scaled_back = gate_col * back
        act[c, dp, :, 0:hidden] = (scaled_back * up_act * slope).astype(BF16)
        act[c, dp, :, hidden : 2 * hidden] = (scaled_back * active).astype(BF16)
        act[c, dp, :, 2 * hidden :] = units
        route = jnp.sum(back * units.astype(F32), axis=1, keepdims=True)
        gates[c] = jnp.zeros((SLOTS, LANES), F32)
        gates[c, pl.ds(pl.multiple_of(dp * PART, PART), PART), :] = jnp.broadcast_to(
            route, (PART, LANES)
        )
        for way in range(2):
            act_copy(0, c, way, act.at[c, dp]).start()

    def pass_act(c):
        for way in range(2):
            source = y_last if way == 0 else y_next
            act_copy(0, c, way, act.at[c, source]).wait_recv()
            act_copy(1, c, way, act.at[c, source, :, columns(way)]).start()

    def half_copy(c):
        return remote(
            row_part.at[c, :, other],
            row_other.at[c],
            half_sem.at[0, c],
            half_sem.at[1, c],
            {"half": other},
        )

    def row_terms(c):
        for way in range(2):
            act_copy(1, c, way, act.at[c, y_far, :, columns(way)]).wait_recv()
        grads = act[c].reshape(SLOTS, three)
        rows = matmul(grads[:, :hidden], w_gate[...], 1, 1) + matmul(
            grads[:, hidden : 2 * hidden], w_up[...], 1, 1
        )
        row_part[c, :, :, :, 0:width] = rows.astype(BF16).reshape(SPAN, 2, UNIT, width)
        row_part[c, :, :, :, width:] = gates[c].astype(BF16).reshape(SPAN, 2, UNIT, LANES)
        half_copy(c).start()

    def back_copy(place, c, j, toward):
        return remote(
            row_send.at[c, j],
            row_back.at[expert],
            back_send.at[place],
            back_recv.at[expert],
            {"expert": toward},
        )

    def give_back(c):
        half_copy(c).wait_recv()
        for j in range(SPAN):
            place = c * SPAN + j
            row_send[c, j] = (
                row_part[c, j, half].astype(F32) + row_other[c, j].astype(F32)
            ).astype(BF16)
            step = div(place + 1, 2)
            offset = step + rem(place + 1, 2) * (RING - 2 * step)
            toward = ring_expert(rem(position + offset, RING), half)

            @pl.when(place != 0)
            def _():
                back_copy(place, c, j, toward).start()

            @pl.when(place == 0)
            def _():
                row_back[expert] = row_send[c, j]

    def weight_terms(c):
        def tile(m, carry):
            span = pl.ds(pl.multiple_of(m * LANES, LANES), LANES)
            acc[span, : 2 * hidden] += matmul(
                slot_x[c, :, span], act[c, :, :, : 2 * hidden].reshape(SLOTS, 2 * hidden), 0, 0
            )
            acc[span, 2 * hidden :] += matmul(
                slot_s[c, :, span], act[c, :, :, 2 * hidden :].reshape(SLOTS, hidden), 0, 0
            )
            return carry

        lax.fori_loop(0, width // LANES, tile, 0)

    def turn(i, carry):
        def staged(lag, work):
            pl.when((i >= lag) & (i - lag < CHUNKS))(functools.partial(work, i - lag))

        staged(0, lambda c: ring_step(2 * c + 1))
        staged(5, row_terms)
        staged(4, pass_act)
        staged(2, add_passing)
        staged(3, activate)

        @pl.when(i < CHUNKS)
        def _():
            ring_step(2 * i + 2)
            give_twin(i)

        staged(1, select)
        staged(6, give_back)
        staged(6, weight_terms)
        return carry

    lax.fori_loop(0, CHUNKS + 6, turn, 0)

    gate_out[...] = acc[:, :hidden].astype(BF16)
    up_out[...] = acc[:, hidden : 2 * hidden].astype(BF16)
    down_out[...] = acc[:, 2 * hidden :].astype(BF16)

    own_gate = own_rows[:, width : width + LANES]
    own_chosen = (own_gate.astype(F32) > 0.0).astype(BF16)
    own_rank = matmul(before_own[...], own_chosen).astype(BF16)
    chosen_at = matmul(own_chosen, spread[...])
    rank_at = matmul(own_rank, spread[...])
    combine = jnp.where(rank_at == slot_of[...], chosen_at, 0.0) * same_part[...]
    combine = combine.astype(BF16)

    def arrival(i, carry):
        source = rem(expert + i, RING)
        remote(
            row_send.at[0, 0],
            row_back.at[source],
            back_send.at[0],
            back_recv.at[source],
            {"expert": source},
        ).wait_recv()
        return carry

    lax.fori_loop(1, RING, arrival, 0)
    returned = row_back[...].reshape(RING * UNIT, width + LANES)
    token_sum = matmul(combine, returned[:, :width])
    route_sum = matmul(combine, returned[:, width:] * gather[...])
    fin_send[:, :, 0:width] = token_sum.astype(BF16).reshape(NY, PAD, width)
    fin_send[:, :, width:] = route_sum.astype(BF16).reshape(NY, PAD, LANES)

    def fin_copy(r):
        return remote(
            fin_send.at[rem(dp + r, NY)],
            fin_recv.at[dp],
            fin_sem.at[0, r],
            fin_sem.at[1, r],
            {"dp": rem(dp + r, NY)},
        )

    def fin_arrival(r):
        source = rem(dp + NY - r, NY)
        return remote(
            fin_send.at[source], fin_recv.at[source], fin_sem.at[0, r], fin_sem.at[1, r], {"dp": source}
        )

    for r in range(1, NY):
        fin_copy(r).start()
    fin_recv[dp] = fin_send[dp]
    for r in range(1, NY):
        fin_arrival(r).wait_recv()
    routes = jnp.zeros((PAD, LANES), F32)
    for q in range(NY):
        token_out[:, q * width : (q + 1) * width] = fin_recv[q, :, 0:width]
        routes = routes + fin_recv[q, :, width:].astype(F32)
    lane = lax.broadcasted_iota(jnp.int32, (PAD, LANES), 1)
    named = jnp.zeros((PAD, LANES), F32)
    for k in range(8):
        value = jnp.sum(jnp.where(ids[:, k : k + 1] == lane, routes, 0.0), axis=1, keepdims=True)
        named = jnp.where(lane == k, value, named)
    route_out[...] = named

    for r in range(1, NY):
        own_copy(r).wait_send()
        fin_copy(r).wait_send()

    def ring_left(step, carry):
        ring_x(step, behind, 0, 1).wait_send()
        ring_d(step, ahead, 0, 1).wait_send()

        @pl.when(step < LAST)
        def _():
            ring_x(step, ahead, 0, 1).wait_send()
            ring_d(step, behind, 0, 1).wait_send()

        return carry

    lax.fori_loop(1, LAST + 1, ring_left, 0)

    def chunk_left(c, carry):
        twin_x(c, half).wait_send()
        twin_d(c, half).wait_send()
        for way in range(2):
            first_sum(c, way).wait_send()
            second_sum(c, way).wait_send()
            act_copy(0, c, way, act.at[c, dp]).wait_send()
            act_copy(1, c, way, act.at[c, y_far, :, columns(way)]).wait_send()
        half_copy(c).wait_send()
        return carry

    lax.fori_loop(0, CHUNKS, chunk_left, 0)

    def back_left(place, carry):
        back_copy(place, 0, 0, ahead).wait_send()
        return carry

    lax.fori_loop(1, RING, back_left, 0)


def constants():
    n = np.arange(TOKENS)
    before_chunk = (n[:, None] // TOK == n[None] // TOK) & (n[:, None] < n[None])
    block, place, micro = n // (SPAN * UNIT_TOK), n // UNIT_TOK % SPAN, n // TOK % NY
    slot_base = np.broadcast_to((place * 2 + block) * UNIT + micro * MOST, (8, TOKENS))
    row, col = np.arange(UNIT_TOK), np.arange(NY * PAD)
    squeeze = (row[:, None] // TOK == col[None] // PAD) & (row[:, None] % TOK == col[None] % PAD)
    before_own = (col[:, None] // PAD == col[None] // PAD) & (col[None] < col[:, None])
    slot = np.arange(RING * UNIT)
    spread = np.arange(LANES)[:, None] == slot[None] // UNIT
    slot_of = np.broadcast_to(slot % MOST, (NY * PAD, RING * UNIT))
    same_part = col[:, None] // PAD == slot[None] // MOST % NY
    return (
        jnp.asarray(before_chunk, BF16),
        jnp.asarray(slot_base, F32),
        jnp.asarray(squeeze, BF16),
        jnp.asarray(before_own, BF16),
        jnp.asarray(spread, BF16),
        jnp.asarray(spread.T, BF16),
        jnp.asarray(slot_of, F32),
        jnp.asarray(same_part, F32),
    )


def on_device(tokens_in, cotangent, expert_ids, gate_probs, gate_weight, up_weight, down_weight):
    half = lax.axis_index("half")
    width, hidden = gate_weight.shape[1], gate_weight.shape[2]

    def block(values):
        return lax.dynamic_index_in_dim(values[0], half, 0, keepdims=False)

    def slices(values):
        return block(values).reshape(TOK, NY, width).transpose(1, 0, 2)

    ids = block(expert_ids)
    named = ids[:, :, None] == jnp.arange(LANES, dtype=jnp.int32)
    gate_map = jnp.sum(jnp.where(named, block(gate_probs).astype(F32)[:, :, None], 0.0), axis=1)
    gate_map = jnp.broadcast_to(gate_map.astype(BF16)[None], (NY, TOK, LANES))
    stage = jnp.concatenate([slices(tokens_in), gate_map, slices(cotangent)], axis=2)
    stage = jnp.pad(stage, ((0, 0), (0, PAD - TOK), (0, 0)))
    ids = jnp.pad(ids, ((0, PAD - TOK), (0, LANES - ids.shape[1])), constant_values=-1)

    vmem = pl.BlockSpec(memory_space=pltpu.VMEM)
    three = 3 * hidden
    weights = jax.ShapeDtypeStruct((width, hidden), BF16)
    out = pl.pallas_call(
        functools.partial(kernel, width, hidden),
        out_shape=(
            jax.ShapeDtypeStruct((PAD, NY * width), BF16),
            jax.ShapeDtypeStruct((PAD, LANES), F32),
            weights,
            weights,
            weights,
        ),
        in_specs=[vmem] * 13,
        out_specs=(vmem,) * 5,
        scratch_shapes=[
            pltpu.VMEM((NY, PAD, 2 * width + LANES), BF16),
            pltpu.VMEM((2, RING, UNIT_TOK, width + LANES), BF16),
            pltpu.VMEM((2, RING, UNIT_TOK, width), BF16),
            pltpu.VMEM((CHUNKS, SLOTS, width), BF16),
            pltpu.VMEM((CHUNKS, SLOTS, width), BF16),
            pltpu.VMEM((CHUNKS, SLOTS, LANES), F32),
            pltpu.VMEM((CHUNKS, NY, PART, three), BF16),
            pltpu.VMEM((CHUNKS, 2, PART, three // 2), BF16),
            pltpu.VMEM((CHUNKS, 2, PART, three), BF16),
            pltpu.VMEM((CHUNKS, NY, PART, three), BF16),
            pltpu.VMEM((CHUNKS, SPAN, 2, UNIT, width + LANES), BF16),
            pltpu.VMEM((CHUNKS, SPAN, UNIT, width + LANES), BF16),
            pltpu.VMEM((CHUNKS, SPAN, UNIT, width + LANES), BF16),
            pltpu.VMEM((RING, UNIT, width + LANES), BF16),
            pltpu.VMEM((NY, PAD, width + LANES), BF16),
            pltpu.VMEM((NY, PAD, width + LANES), BF16),
            pltpu.VMEM((width, three), F32),
            pltpu.SemaphoreType.DMA((2, NY)),
            pltpu.SemaphoreType.DMA((2, 2, 2, LAST)),
            pltpu.SemaphoreType.DMA((2, 2, CHUNKS)),
            pltpu.SemaphoreType.DMA((2, 2, 2, CHUNKS)),
            pltpu.SemaphoreType.DMA((2, 2, 2, CHUNKS)),
            pltpu.SemaphoreType.DMA((2, CHUNKS)),
            pltpu.SemaphoreType.DMA((RING,)),
            pltpu.SemaphoreType.DMA((RING,)),
            pltpu.SemaphoreType.DMA((2, NY)),
        ],
        compiler_params=pltpu.CompilerParams(
            collective_id=0, has_side_effects=True, vmem_limit_bytes=62 * 1024 * 1024
        ),
    )(stage, gate_weight[0], up_weight[0], down_weight[0], ids, *constants())
    token_rows, route_rows, gate_grad, up_grad, down_grad = out
    token_grad = token_rows[:TOK][None, None]
    route_grad = route_rows[:TOK, : expert_ids.shape[3]].astype(BF16)[None, None]
    return token_grad, route_grad, gate_grad[None], up_grad[None], down_grad[None]


def solution(mesh):
    return jax.shard_map(
        on_device,
        mesh=mesh,
        in_specs=(
            P(("expert", "dp"), None, None, None),
            P(("expert", "dp"), None, None, None),
            P(("expert", "dp"), None, None, None),
            P(("expert", "dp"), None, None, None),
            P("expert", "dp", "half"),
            P("expert", "dp", "half"),
            P("expert", "dp", "half"),
        ),
        out_specs=(
            P(("expert", "dp"), "half", None, None),
            P(("expert", "dp"), "half", None, None),
            P("expert", "dp", "half"),
            P("expert", "dp", "half"),
            P("expert", "dp", "half"),
        ),
        check_vma=False,
    )
```

```python
import functools

import jax
import jax.numpy as jnp
from jax import lax
from jax.experimental import pallas as pl
from jax.experimental.pallas import tpu as pltpu
from jax.sharding import PartitionSpec as P

MESH = pl.DeviceIdType.MESH
BF16 = jnp.bfloat16
F32 = jnp.float32

MOST = 6
TOK = 12
PAD = 16
NX, NY, NZ = 4, 4, 8
RING = NX * NZ
LAST = NZ // 2
SPAN = 2
CHUNKS = RING // SPAN
UNIT_TOK = NY * TOK
UNIT = NY * MOST
TOKENS = 2 * SPAN * UNIT_TOK
SLOTS = 2 * SPAN * UNIT
PART = SLOTS // NY
LANES = 128


def rem(a, b):
    return lax.rem(a, jnp.int32(b))


def div(a, b):
    return lax.div(a, jnp.int32(b))


def choose(index, values):
    found = jnp.int32(values[0])
    for i, value in enumerate(values[1:], 1):
        if value != values[0]:
            found = jnp.where(index == i, jnp.int32(value), found)
    return found


Z_ORDER = (0, 1, 7, 2, 6, 3, 5, 4)
FIRST_Z = (0, 0, 1, 7, 1, 7, 2, 6, 2, 6, 3, 5, 3, 5, 4, 4)
FIRST_X = (0, 1, 0, 0, 1, 1, 0, 0, 1, 1, 0, 0, 1, 1, 0, 1)
SECOND_X = (0, 0, 0, 0, 1, 3, 1, 3, 1, 3, 1, 3, 2, 2, 2, 2)
SECOND_Z = (0, 1, 2, 3, 0, 0, 1, 1, 2, 2, 3, 3, 0, 1, 2, 3)


def order(n):
    return jnp.where(n < 4, n, jnp.where(n == CHUNKS - 1, 4, n + 1))


def owner(expert, half, c, j):
    x, z = div(expert, NZ), rem(expert, NZ)
    first = rem(x + choose(c, FIRST_X) * SPAN + j, NX) * NZ + rem(z + choose(c, FIRST_Z), NZ)
    z_step = choose(choose(c, SECOND_Z) * SPAN + j, Z_ORDER)
    second = rem(x + choose(c, SECOND_X), NX) * NZ + rem(z + z_step, NZ)
    return first + half * (second - first)


def index_of(shape, dim):
    return lax.broadcasted_iota(jnp.int32, shape, dim).astype(F32)


def whole(number, size):
    return jnp.floor((number + 0.5) * (1.0 / size))


def part_of(number, size):
    return number - size * whole(number, size)


def before(size, span):
    row, col = index_of((size, size), 0), index_of((size, size), 1)
    return jnp.where((whole(row, span) == whole(col, span)) & (row < col), 1.0, 0.0).astype(BF16)


def matmul(a, b, a_dim=1, b_dim=0):
    return lax.dot_general(a, b, (((a_dim,), (b_dim,)), ((), ())), preferred_element_type=F32)


def kernel(
    width,
    hidden,
    stage,
    w_gate_hbm,
    w_up_hbm,
    w_down_hbm,
    ids,
    token_out,
    route_out,
    grads_hbm,
    w_gate,
    w_up,
    w_down,
    before_chunk,
    own,
    unit_x,
    unit_d,
    slot_x,
    slot_s,
    gates,
    part,
    sum_one,
    sum_two,
    act,
    row_part,
    row_other,
    row_send,
    row_back,
    fin_send,
    fin_recv,
    acc,
    grads_out,
    own_sem,
    near_sem,
    far_sem,
    twin_sem,
    sum_sem,
    act_sem,
    half_sem,
    back_send,
    back_recv,
    fin_sem,
    load_sem,
):
    loads = [
        pltpu.make_async_copy(src, dst, load_sem.at[n])
        for n, (src, dst) in enumerate(((w_gate_hbm, w_gate), (w_up_hbm, w_up), (w_down_hbm, w_down)))
    ]
    for load in loads:
        load.start()
    expert, half, dp = lax.axis_index("expert"), lax.axis_index("half"), lax.axis_index("dp")
    other = 1 - half
    x, z = div(expert, NZ), rem(expert, NZ)
    z_next, z_last = x * NZ + rem(z + 1, NZ), x * NZ + rem(z + NZ - 1, NZ)
    z_two_next, z_two_last = x * NZ + rem(z + 2, NZ), x * NZ + rem(z + NZ - 2, NZ)
    x_at = [rem(x + r, NX) * NZ + z for r in range(NX)]
    y_next, y_last, y_far = rem(dp + 1, NY), rem(dp + 3, NY), rem(dp + 2, NY)
    three = 3 * hidden
    mid = three // 2

    def remote(src, dst, send, recv, where):
        return pltpu.make_async_remote_copy(
            src_ref=src, dst_ref=dst, send_sem=send, recv_sem=recv, device_id=where, device_id_type=MESH
        )

    barrier = pltpu.get_barrier_semaphore()

    def greet(i, carry):
        pl.semaphore_signal(
            barrier, inc=1, device_id={"expert": rem(expert + i, RING)}, device_id_type=MESH
        )
        return carry

    lax.fori_loop(1, RING, greet, 0)
    for r in range(1, NY):
        pl.semaphore_signal(barrier, inc=1, device_id={"dp": rem(dp + r, NY)}, device_id_type=MESH)
    pl.semaphore_signal(barrier, inc=1, device_id={"half": other}, device_id_type=MESH)
    acc[...] = jnp.zeros_like(acc)
    before_chunk[...] = before(TOKENS, TOK)
    own[dp] = stage[dp]
    row, col = index_of((UNIT_TOK, NY * PAD), 0), index_of((UNIT_TOK, NY * PAD), 1)
    same = (whole(row, TOK) == whole(col, PAD)) & (part_of(row, TOK) == part_of(col, PAD))
    squeeze = jnp.where(same, 1.0, 0.0).astype(BF16)
    pl.semaphore_wait(barrier, RING - 1 + NY - 1 + 1)

    def own_copy(r):
        return remote(
            stage.at[rem(dp + r, NY)],
            own.at[dp],
            own_sem.at[0, r],
            own_sem.at[1, r],
            {"dp": rem(dp + r, NY)},
        )

    def own_arrival(r):
        source = rem(dp + NY - r, NY)
        return remote(stage.at[source], own.at[source], own_sem.at[0, r], own_sem.at[1, r], {"dp": source})

    for r in range(1, NY):
        own_copy(r).start()
    for r in range(1, NY):
        own_arrival(r).wait_recv()
    own_rows = own[...].reshape(NY * PAD, 2 * width + LANES)
    packed = matmul(squeeze, own_rows).astype(BF16)
    unit_x[half, 0] = packed[:, : width + LANES]
    unit_d[half, 0] = packed[:, width + LANES :]

    units = (unit_x, unit_d)

    def near(kind, src, dst, toward):
        return remote(
            units[kind].at[half, src],
            units[kind].at[half, dst],
            near_sem.at[kind, 0, dst],
            near_sem.at[kind, 1, dst],
            {"expert": toward},
        )

    def far(kind, src, dst, toward):
        return remote(
            units[kind].at[half, pl.ds(src * SPAN, SPAN)],
            units[kind].at[half, pl.ds(dst * SPAN, SPAN)],
            far_sem.at[kind, 0, dst],
            far_sem.at[kind, 1, dst],
            {"expert": toward},
        )

    def near_wait(dst):
        for kind in range(2):
            near(kind, dst, dst, z_next).wait_recv()

    def near_pass(src, dst, toward):
        for kind in range(2):
            near(kind, src, dst, toward).start()

    def far_wait(dst):
        for kind in range(2):
            far(kind, dst, dst, z_next).wait_recv()

    def far_pass(src, dst, toward):
        for kind in range(2):
            far(kind, src, dst, toward).start()

    @pl.when(half == 0)
    def _():
        near_pass(0, 1, x_at[3])
        near_pass(0, 3, x_at[1])

    @pl.when(half == 1)
    def _():
        near_pass(0, 1, z_last)
        near_pass(0, 2, z_next)

    def take_first(c):
        @pl.when(c == 0)
        def _():
            near_wait(1)
            near_pass(0, 2, x_at[2])

        @pl.when(c == 1)
        def _():
            near_wait(3)
            near_wait(2)

        @pl.when(c > 1)
        def _():
            far_wait(c)

        @pl.when(c < 2)
        def _():
            far_pass(c, 2 * c + 2, z_last)
            far_pass(c, 2 * c + 3, z_next)

        even = rem(c, 2) == 0

        @pl.when((c > 1) & (c < 11) & even)
        def _():
            far_pass(c, c + 4, z_last)

        @pl.when((c > 1) & (c < 10) & jnp.logical_not(even))
        def _():
            far_pass(c, c + 4, z_next)

        @pl.when(c == 13)
        def _():
            far_pass(c, 15, z_next)

    def take_second(c):
        @pl.when(c == 0)
        def _():
            near_wait(1)
            near_pass(0, 3, z_two_last)
            near_pass(0, 4, z_two_next)

        @pl.when(c == 1)
        def _():
            near_wait(2)
            near_wait(3)
            near_pass(3, 5, z_last)

        @pl.when(c == 2)
        def _():
            near_wait(4)
            near_pass(4, 6, z_next)
            near_wait(5)
            near(0, 5, 7, z_last).start()

        @pl.when(c == 3)
        def _():
            near_wait(6)
            near(1, 6, 7, z_next).start()
            near_wait(7)

        @pl.when(c > 3)
        def _():
            far_wait(c)

        @pl.when(c < 4)
        def _():
            far_pass(c, 2 * c + 4, x_at[3])
            far_pass(c, 2 * c + 5, x_at[1])

        @pl.when((c == 4) | (c == 6))
        def _():
            far_pass(c, 10 + div(c, 2), x_at[3])

        @pl.when((c == 9) | (c == 11))
        def _():
            far_pass(c, 10 + div(c, 2), x_at[1])

    def take(c):
        pl.when(half == 0)(functools.partial(take_first, c))
        pl.when(half == 1)(functools.partial(take_second, c))
        twin_x(c, half).start()
        twin_d(c, half).start()

    def twin_x(c, block):
        span = pl.ds(c * SPAN, SPAN)
        return remote(
            unit_x.at[block, span],
            unit_x.at[block, span],
            twin_sem.at[0, 0, c],
            twin_sem.at[0, 1, c],
            {"half": other},
        )

    def twin_d(c, block):
        span = pl.ds(c * SPAN, SPAN)
        return remote(
            unit_d.at[block, span],
            unit_d.at[block, span],
            twin_sem.at[1, 0, c],
            twin_sem.at[1, 1, c],
            {"half": other},
        )

    def sum_copy(stage_no, c, way, src, dst):
        return remote(
            src,
            dst,
            sum_sem.at[stage_no, 0, way, c],
            sum_sem.at[stage_no, 1, way, c],
            {"dp": y_next if way == 0 else y_last},
        )

    def act_copy(stage_no, c, way, view):
        return remote(
            view,
            view,
            act_sem.at[stage_no, 0, way, c],
            act_sem.at[stage_no, 1, way, c],
            {"dp": y_next if way == 0 else y_last},
        )

    def columns(way):
        return pl.ds(way * mid, mid)

    def first_sum(c, way):
        return sum_copy(0, c, way, part.at[c, y_far, :, columns(way)], sum_one.at[c, way])

    def second_sum(c, way):
        toward = y_next if way == 0 else y_last
        return sum_copy(1, c, way, part.at[c, toward], sum_two.at[c, way])

    def select(c):
        chunk = order(c)
        twin_x(chunk, other).wait_recv()
        twin_d(chunk, other).wait_recv()
        span = pl.ds(chunk * SPAN, SPAN)
        block_x = [unit_x[b, span].reshape(SPAN * UNIT_TOK, width + LANES) for b in range(2)]
        all_x = jnp.concatenate(block_x, axis=0)
        is_expert = lax.broadcasted_iota(jnp.int32, (8, LANES), 1) == expert
        gate_row = matmul(is_expert.astype(BF16), all_x[:, width:], 1, 1)
        chosen = gate_row > 0.0
        rank = matmul(chosen.astype(BF16), before_chunk[...])
        token = index_of((8, TOKENS), 1)
        unit = whole(token, UNIT_TOK)
        unit = part_of(unit, SPAN) * 2 + whole(unit, SPAN)
        base = unit * UNIT + part_of(whole(token, TOK), NY) * MOST
        place = jnp.where(chosen, base + rank, -1.0)
        pick = jnp.where(index_of((SLOTS, TOKENS), 0) == place[:1], 1.0, 0.0).astype(BF16)
        gate_wide = matmul(
            pick, jnp.broadcast_to(gate_row[:1], (LANES, TOKENS)).astype(BF16), 1, 1
        )
        gates[c] = gate_wide
        slots = matmul(pick, all_x[:, :width]).astype(BF16)
        slot_x[c] = slots
        block_d = [unit_d[b, span].reshape(SPAN * UNIT_TOK, width) for b in range(2)]
        slots_d = matmul(pick, jnp.concatenate(block_d, axis=0))
        slot_s[c] = (gate_wide[:, :1] * slots_d).astype(BF16)
        shape = (NY, PART, hidden)
        part[c, :, :, 0:hidden] = matmul(slots, w_gate[...]).astype(BF16).reshape(shape)
        part[c, :, :, hidden : 2 * hidden] = matmul(slots, w_up[...]).astype(BF16).reshape(shape)
        part[c, :, :, 2 * hidden :] = (
            matmul(slots_d.astype(BF16), w_down[...]).astype(BF16).reshape(shape)
        )
        for way in range(2):
            first_sum(c, way).start()

    def add_passing(c):
        for way in range(2):
            first_sum(c, way).wait_recv()
            toward = y_next if way == 0 else y_last
            here = part[c, toward, :, columns(way)].astype(F32)
            part[c, toward, :, columns(way)] = (here + sum_one[c, way].astype(F32)).astype(BF16)
            second_sum(c, way).start()

    def activate(c):
        for way in range(2):
            second_sum(c, way).wait_recv()
        summed = (
            part[c, dp].astype(F32) + sum_two[c, 0].astype(F32) + sum_two[c, 1].astype(F32)
        )
        gate_act, up_act, back = (
            summed[:, :hidden],
            summed[:, hidden : 2 * hidden],
            summed[:, 2 * hidden :],
        )
        gate_col = gates[c, pl.ds(pl.multiple_of(dp * PART, PART), PART), :][:, :1]
        sigma = jax.nn.sigmoid(gate_act)
        active = gate_act * sigma
        slope = sigma * (1.0 + gate_act * (1.0 - sigma))
        units = (active * up_act).astype(BF16)
        scaled_back = gate_col * back
        act[c, dp, :, 0:hidden] = (scaled_back * up_act * slope).astype(BF16)
        act[c, dp, :, hidden : 2 * hidden] = (scaled_back * active).astype(BF16)
        act[c, dp, :, 2 * hidden :] = units
        route = jnp.sum(back * units.astype(F32), axis=1, keepdims=True)
        gates[c] = jnp.zeros((SLOTS, LANES), F32)
        gates[c, pl.ds(pl.multiple_of(dp * PART, PART), PART), :] = jnp.broadcast_to(
            route, (PART, LANES)
        )
        for way in range(2):
            act_copy(0, c, way, act.at[c, dp]).start()

    def pass_act(c):
        for way in range(2):
            source = y_last if way == 0 else y_next
            act_copy(0, c, way, act.at[c, source]).wait_recv()
            act_copy(1, c, way, act.at[c, source, :, columns(way)]).start()

    def half_copy(c):
        return remote(
            row_part.at[c, :, other],
            row_other.at[c],
            half_sem.at[0, c],
            half_sem.at[1, c],
            {"half": other},
        )

    def row_terms(c):
        for way in range(2):
            act_copy(1, c, way, act.at[c, y_far, :, columns(way)]).wait_recv()
        grads = act[c].reshape(SLOTS, three)
        rows = matmul(grads[:, :hidden], w_gate[...], 1, 1) + matmul(
            grads[:, hidden : 2 * hidden], w_up[...], 1, 1
        )
        row_part[c, :, :, :, 0:width] = rows.astype(BF16).reshape(SPAN, 2, UNIT, width)
        row_part[c, :, :, :, width:] = gates[c].astype(BF16).reshape(SPAN, 2, UNIT, LANES)
        half_copy(c).start()

    def back_copy(place, c, j, toward):
        return remote(
            row_send.at[c, j],
            row_back.at[expert],
            back_send.at[place],
            back_recv.at[expert],
            {"expert": toward},
        )

    def give_back(c):
        half_copy(c).wait_recv()
        for j in range(SPAN):
            place = c * SPAN + j
            row_send[c, j] = (
                row_part[c, j, half].astype(F32) + row_other[c, j].astype(F32)
            ).astype(BF16)
            toward = owner(expert, half, order(c), j)

            @pl.when(place != 0)
            def _():
                back_copy(place, c, j, toward).start()

            @pl.when(place == 0)
            def _():
                row_back[expert] = row_send[c, j]

    def weight_terms(c):
        pair = pl.ds(c - 1, 2)

        def tile(m, carry):
            span = pl.ds(pl.multiple_of(m * LANES, LANES), LANES)
            acc[span, : 2 * hidden] += matmul(
                slot_x[pair, :, span].reshape(2 * SLOTS, LANES),
                act[pair, :, :, : 2 * hidden].reshape(2 * SLOTS, 2 * hidden),
                0,
                0,
            )
            acc[span, 2 * hidden :] += matmul(
                slot_s[pair, :, span].reshape(2 * SLOTS, LANES),
                act[pair, :, :, 2 * hidden :].reshape(2 * SLOTS, hidden),
                0,
                0,
            )
            return carry

        @pl.when(rem(c, 2) == 1)
        def _():
            lax.fori_loop(0, width // LANES, tile, 0)

    for load in loads:
        load.wait()

    def turn(i, carry):
        def staged(lag, work):
            pl.when((i >= lag) & (i - lag < CHUNKS))(functools.partial(work, i - lag))

        staged(7, pass_act)
        staged(5, activate)
        staged(3, add_passing)
        staged(1, select)
        first = i + jnp.where(i > 4, 1, 0)
        beyond = jnp.minimum(i + 1 + jnp.where(i > 3, 1, 0), CHUNKS)

        def take_one(c, carry):
            take(c)
            return carry

        lax.fori_loop(first, beyond, take_one, 0)
        staged(9, row_terms)
        staged(10, give_back)
        staged(11, weight_terms)
        return carry

    lax.fori_loop(0, CHUNKS + 11, turn, 0)

    own_gate = own_rows[:, width : width + LANES]
    own_chosen = (own_gate.astype(F32) > 0.0).astype(BF16)
    own_rank = matmul(before(NY * PAD, PAD), own_chosen, 0, 0).astype(BF16)
    returns = RING * UNIT
    spread = jnp.where(
        index_of((LANES, returns), 0) == whole(index_of((LANES, returns), 1), UNIT), 1.0, 0.0
    ).astype(BF16)
    chosen_at = matmul(own_chosen, spread)
    rank_at = matmul(own_rank, spread)
    own_token, slot = index_of((NY * PAD, returns), 0), index_of((NY * PAD, returns), 1)
    fits = (rank_at == part_of(slot, MOST)) & (
        whole(own_token, PAD) == part_of(whole(slot, MOST), NY)
    )
    combine = jnp.where(fits, chosen_at, 0.0).astype(BF16)
    gather = jnp.where(
        whole(index_of((returns, LANES), 0), UNIT) == index_of((returns, LANES), 1), 1.0, 0.0
    ).astype(BF16)

    def arrival(i, carry):
        source = rem(expert + i, RING)
        remote(
            row_send.at[0, 0],
            row_back.at[source],
            back_send.at[0],
            back_recv.at[source],
            {"expert": source},
        ).wait_recv()
        return carry

    lax.fori_loop(1, RING, arrival, 0)
    returned = row_back[...].reshape(RING * UNIT, width + LANES)
    token_sum = matmul(combine, returned[:, :width])
    route_sum = matmul(combine, returned[:, width:] * gather)
    fin_send[:, :, 0:width] = token_sum.astype(BF16).reshape(NY, PAD, width)
    fin_send[:, :, width:] = route_sum.astype(BF16).reshape(NY, PAD, LANES)

    def fin_copy(r):
        return remote(
            fin_send.at[rem(dp + r, NY)],
            fin_recv.at[dp],
            fin_sem.at[0, r],
            fin_sem.at[1, r],
            {"dp": rem(dp + r, NY)},
        )

    def fin_arrival(r):
        source = rem(dp + NY - r, NY)
        return remote(
            fin_send.at[source], fin_recv.at[source], fin_sem.at[0, r], fin_sem.at[1, r], {"dp": source}
        )

    for r in range(1, NY):
        fin_copy(r).start()
    fin_recv[dp] = fin_send[dp]
    for n in range(3):
        grads_out[n] = acc[:, n * hidden : (n + 1) * hidden].astype(BF16)
    store = pltpu.make_async_copy(grads_out, grads_hbm, load_sem.at[3])
    store.start()
    for r in range(1, NY):
        fin_arrival(r).wait_recv()
    routes = jnp.zeros((PAD, LANES), F32)
    for q in range(NY):
        token_out[:, q * width : (q + 1) * width] = fin_recv[q, :, 0:width]
        routes = routes + fin_recv[q, :, width:].astype(F32)
    lane = lax.broadcasted_iota(jnp.int32, (PAD, LANES), 1)
    named = jnp.zeros((PAD, LANES), F32)
    for k in range(8):
        value = jnp.sum(jnp.where(ids[:, k : k + 1] == lane, routes, 0.0), axis=1, keepdims=True)
        named = jnp.where(lane == k, value, named)
    route_out[...] = named

    store.wait()
    for r in range(1, NY):
        own_copy(r).wait_send()
        fin_copy(r).wait_send()

    for kind in range(2):
        for dst in range(1, NX):
            near(kind, 0, dst, z_next).wait_send()

        @pl.when(half == 0)
        def _(kind=kind):
            far(kind, 0, 2, z_next).wait_send()
            far(kind, 0, 3, z_next).wait_send()

        @pl.when(half == 1)
        def _(kind=kind):
            for dst in range(NX, NZ):
                near(kind, 0, dst, z_next).wait_send()

        for dst in range(4, CHUNKS):
            far(kind, 0, dst, z_next).wait_send()

    def chunk_left(c, carry):
        twin_x(c, half).wait_send()
        twin_d(c, half).wait_send()
        for way in range(2):
            first_sum(c, way).wait_send()
            second_sum(c, way).wait_send()
            act_copy(0, c, way, act.at[c, dp]).wait_send()
            act_copy(1, c, way, act.at[c, y_far, :, columns(way)]).wait_send()
        half_copy(c).wait_send()
        return carry

    lax.fori_loop(0, CHUNKS, chunk_left, 0)

    def back_left(place, carry):
        back_copy(place, 0, 0, z_next).wait_send()
        return carry

    lax.fori_loop(1, RING, back_left, 0)


def finish(token_rows, route_rows, grads, token_out, route_out, gate_out, up_out, down_out, sem):
    copies = [
        pltpu.make_async_copy(grads.at[n], target.at[0], sem.at[n])
        for n, target in enumerate((gate_out, up_out, down_out))
    ]
    for copy in copies:
        copy.start()
    token_out[0, 0] = token_rows[:TOK]
    route_out[0, 0] = route_rows[:TOK, : route_out.shape[3]].astype(BF16)
    for copy in copies:
        copy.wait()


def on_device(tokens_in, cotangent, expert_ids, gate_probs, gate_weight, up_weight, down_weight):
    half = lax.axis_index("half")
    width, hidden = gate_weight.shape[1], gate_weight.shape[2]

    def block(values):
        return jnp.where(half == 0, values[0, 0], values[0, 1])

    def slices(values):
        return block(values).reshape(TOK, NY, width).transpose(1, 0, 2)

    ids = block(expert_ids)
    named = ids[:, :, None] == jnp.arange(LANES, dtype=jnp.int32)
    gate_map = jnp.sum(jnp.where(named, block(gate_probs).astype(F32)[:, :, None], 0.0), axis=1)
    gate_map = jnp.broadcast_to(gate_map.astype(BF16)[None], (NY, TOK, LANES))
    stage = jnp.concatenate([slices(tokens_in), gate_map, slices(cotangent)], axis=2)
    stage = jnp.pad(stage, ((0, 0), (0, PAD - TOK), (0, 0)))
    ids = jnp.pad(ids, ((0, PAD - TOK), (0, LANES - ids.shape[1])), constant_values=-1)

    vmem = pl.BlockSpec(memory_space=pltpu.VMEM)
    hbm = pl.BlockSpec(memory_space=pl.ANY)
    three = 3 * hidden
    weights = jax.ShapeDtypeStruct((1, width, hidden), BF16)
    out = pl.pallas_call(
        functools.partial(kernel, width, hidden),
        out_shape=(
            jax.ShapeDtypeStruct((PAD, NY * width), BF16),
            jax.ShapeDtypeStruct((PAD, LANES), F32),
            jax.ShapeDtypeStruct((3, width, hidden), BF16),
        ),
        in_specs=[vmem] + [hbm] * 3 + [vmem],
        out_specs=(vmem, vmem, hbm),
        scratch_shapes=[
            *[pltpu.VMEM((width, hidden), BF16)] * 3,
            pltpu.VMEM((TOKENS, TOKENS), BF16),
            pltpu.VMEM((NY, PAD, 2 * width + LANES), BF16),
            pltpu.VMEM((2, RING, UNIT_TOK, width + LANES), BF16),
            pltpu.VMEM((2, RING, UNIT_TOK, width), BF16),
            pltpu.VMEM((CHUNKS, SLOTS, width), BF16),
            pltpu.VMEM((CHUNKS, SLOTS, width), BF16),
            pltpu.VMEM((CHUNKS, SLOTS, LANES), F32),
            pltpu.VMEM((CHUNKS, NY, PART, three), BF16),
            pltpu.VMEM((CHUNKS, 2, PART, three // 2), BF16),
            pltpu.VMEM((CHUNKS, 2, PART, three), BF16),
            pltpu.VMEM((CHUNKS, NY, PART, three), BF16),
            pltpu.VMEM((CHUNKS, SPAN, 2, UNIT, width + LANES), BF16),
            pltpu.VMEM((CHUNKS, SPAN, UNIT, width + LANES), BF16),
            pltpu.VMEM((CHUNKS, SPAN, UNIT, width + LANES), BF16),
            pltpu.VMEM((RING, UNIT, width + LANES), BF16),
            pltpu.VMEM((NY, PAD, width + LANES), BF16),
            pltpu.VMEM((NY, PAD, width + LANES), BF16),
            pltpu.VMEM((width, three), F32),
            pltpu.VMEM((3, width, hidden), BF16),
            pltpu.SemaphoreType.DMA((2, NY)),
            pltpu.SemaphoreType.DMA((2, 2, NZ)),
            pltpu.SemaphoreType.DMA((2, 2, CHUNKS)),
            pltpu.SemaphoreType.DMA((2, 2, CHUNKS)),
            pltpu.SemaphoreType.DMA((2, 2, 2, CHUNKS)),
            pltpu.SemaphoreType.DMA((2, 2, 2, CHUNKS)),
            pltpu.SemaphoreType.DMA((2, CHUNKS)),
            pltpu.SemaphoreType.DMA((RING,)),
            pltpu.SemaphoreType.DMA((RING,)),
            pltpu.SemaphoreType.DMA((2, NY)),
            pltpu.SemaphoreType.DMA((4,)),
        ],
        compiler_params=pltpu.CompilerParams(
            collective_id=0, has_side_effects=True, vmem_limit_bytes=62 * 1024 * 1024
        ),
    )(stage, gate_weight[0], up_weight[0], down_weight[0], ids)
    return pl.pallas_call(
        finish,
        out_shape=(
            jax.ShapeDtypeStruct((1, 1, TOK, NY * width), BF16),
            jax.ShapeDtypeStruct((1, 1, TOK, expert_ids.shape[3]), BF16),
            weights,
            weights,
            weights,
        ),
        in_specs=[vmem, vmem, hbm],
        out_specs=(vmem, vmem, hbm, hbm, hbm),
        scratch_shapes=[pltpu.SemaphoreType.DMA((3,))],
    )(*out)


def solution(mesh):
    return jax.shard_map(
        on_device,
        mesh=mesh,
        in_specs=(
            P(("expert", "dp"), None, None, None),
            P(("expert", "dp"), None, None, None),
            P(("expert", "dp"), None, None, None),
            P(("expert", "dp"), None, None, None),
            P("expert", "dp", "half"),
            P("expert", "dp", "half"),
            P("expert", "dp", "half"),
        ),
        out_specs=(
            P(("expert", "dp"), "half", None, None),
            P(("expert", "dp"), "half", None, None),
            P("expert", "dp", "half"),
            P("expert", "dp", "half"),
            P("expert", "dp", "half"),
        ),
        check_vma=False,
    )
```

```python
import functools

import jax
import jax.numpy as jnp
from jax import lax
from jax.experimental import pallas as pl
from jax.experimental.pallas import tpu as pltpu
from jax.sharding import PartitionSpec as P

MESH = pl.DeviceIdType.MESH
BF16 = jnp.bfloat16
F32 = jnp.float32

TOP = 8
MOST = 6
TOK = 12
PAD = 16
NX, NY, NZ = 4, 4, 8
RING = NX * NZ
LAST = NZ // 2
SPAN = 2
CHUNKS = RING // SPAN
UNIT_TOK = NY * TOK
UNIT = NY * MOST
TOKENS = 2 * SPAN * UNIT_TOK
SLOTS = 2 * SPAN * UNIT
PART = SLOTS // NY
LANES = 128


def rem(a, b):
    return lax.rem(a, jnp.int32(b))


def div(a, b):
    return lax.div(a, jnp.int32(b))


def choose(index, values):
    found = jnp.int32(values[0])
    for i, value in enumerate(values[1:], 1):
        if value != values[0]:
            found = jnp.where(index == i, jnp.int32(value), found)
    return found


Z_ORDER = (0, 1, 7, 2, 6, 3, 5, 4)
FIRST_Z = (0, 0, 1, 7, 1, 7, 2, 6, 2, 6, 3, 5, 3, 5, 4, 4)
FIRST_X = (0, 1, 0, 0, 1, 1, 0, 0, 1, 1, 0, 0, 1, 1, 0, 1)
SECOND_X = (0, 0, 0, 0, 1, 3, 1, 3, 1, 3, 1, 3, 2, 2, 2, 2)
SECOND_Z = (0, 1, 2, 3, 0, 0, 1, 1, 2, 2, 3, 3, 0, 1, 2, 3)


def order(n):
    return jnp.where(n < 4, n, jnp.where(n == CHUNKS - 1, 4, n + 1))


def owner(expert, half, c, j):
    x, z = div(expert, NZ), rem(expert, NZ)
    first = rem(x + choose(c, FIRST_X) * SPAN + j, NX) * NZ + rem(z + choose(c, FIRST_Z), NZ)
    z_step = choose(choose(c, SECOND_Z) * SPAN + j, Z_ORDER)
    second = rem(x + choose(c, SECOND_X), NX) * NZ + rem(z + z_step, NZ)
    return first + half * (second - first)


def index_of(shape, dim):
    return lax.broadcasted_iota(jnp.int32, shape, dim).astype(F32)


def whole(number, size):
    return jnp.floor((number + 0.5) * (1.0 / size))


def part_of(number, size):
    return number - size * whole(number, size)


def before(size, span):
    row, col = index_of((size, size), 0), index_of((size, size), 1)
    return jnp.where((whole(row, span) == whole(col, span)) & (row < col), 1.0, 0.0).astype(BF16)


def matmul(a, b, a_dim=1, b_dim=0):
    return lax.dot_general(a, b, (((a_dim,), (b_dim,)), ((), ())), preferred_element_type=F32)


def kernel(
    width,
    hidden,
    tokens,
    cotangent,
    ids,
    probs,
    w_gate_hbm,
    w_up_hbm,
    w_down_hbm,
    token_out,
    route_out,
    grads_hbm,
    w_gate,
    w_up,
    w_down,
    before_chunk,
    stage,
    own,
    units,
    slot_x,
    slot_s,
    gates,
    part,
    sum_one,
    sum_two,
    act,
    row_part,
    row_other,
    row_send,
    row_back,
    fin_send,
    fin_recv,
    acc,
    grads_out,
    own_sem,
    near_sem,
    far_sem,
    twin_sem,
    sum_sem,
    act_sem,
    half_sem,
    back_send,
    back_recv,
    fin_sem,
    load_sem,
):
    loads = [
        pltpu.make_async_copy(src, dst, load_sem.at[n])
        for n, (src, dst) in enumerate(((w_gate_hbm, w_gate), (w_up_hbm, w_up), (w_down_hbm, w_down)))
    ]
    for load in loads:
        load.start()
    expert, half, dp = lax.axis_index("expert"), lax.axis_index("half"), lax.axis_index("dp")
    other = 1 - half
    x, z = div(expert, NZ), rem(expert, NZ)
    z_next, z_last = x * NZ + rem(z + 1, NZ), x * NZ + rem(z + NZ - 1, NZ)
    z_two_next, z_two_last = x * NZ + rem(z + 2, NZ), x * NZ + rem(z + NZ - 2, NZ)
    x_at = [rem(x + r, NX) * NZ + z for r in range(NX)]
    y_next, y_last, y_far = rem(dp + 1, NY), rem(dp + 3, NY), rem(dp + 2, NY)
    three = 3 * hidden
    mid = three // 2

    def remote(src, dst, send, recv, where):
        return pltpu.make_async_remote_copy(
            src_ref=src, dst_ref=dst, send_sem=send, recv_sem=recv, device_id=where, device_id_type=MESH
        )

    barrier = pltpu.get_barrier_semaphore()

    def greet(i, carry):
        pl.semaphore_signal(
            barrier, inc=1, device_id={"expert": rem(expert + i, RING)}, device_id_type=MESH
        )
        return carry

    lax.fori_loop(1, RING, greet, 0)
    for r in range(1, NY):
        pl.semaphore_signal(barrier, inc=1, device_id={"dp": rem(dp + r, NY)}, device_id_type=MESH)
    pl.semaphore_signal(barrier, inc=1, device_id={"half": other}, device_id_type=MESH)
    acc[...] = jnp.zeros_like(acc)
    before_chunk[...] = before(TOKENS, TOK)
    row, col = index_of((PAD, 2 * TOK), 0), index_of((PAD, 2 * TOK), 1)
    mine = jnp.where((row < TOK) & (col == 2 * row + half), 1.0, 0.0).astype(BF16)
    block_x = matmul(mine, tokens[...].reshape(2 * TOK, NY * width)).astype(BF16)
    block_d = matmul(mine, cotangent[...].reshape(2 * TOK, NY * width)).astype(BF16)
    named, weight = ids[half], probs[half].astype(F32)
    lane = lax.broadcasted_iota(jnp.int32, (LANES, TOK), 0)
    gate_map = jnp.zeros((LANES, TOK), F32)
    for k in range(TOP):
        gate_map = jnp.where(named[k : k + 1] == lane, weight[k : k + 1], gate_map)
    unit = jnp.where(index_of((PAD, TOK), 0) == index_of((PAD, TOK), 1), 1.0, 0.0).astype(BF16)
    gate_map = matmul(unit, gate_map.astype(BF16), 1, 1).astype(BF16)
    for q in range(NY):
        stage[q, :, 0:width] = block_x[:, q * width : (q + 1) * width]
        stage[q, :, width : width + LANES] = gate_map
        stage[q, :, width + LANES :] = block_d[:, q * width : (q + 1) * width]
    own[dp] = stage[dp]
    row, col = index_of((UNIT_TOK, NY * PAD), 0), index_of((UNIT_TOK, NY * PAD), 1)
    same = (whole(row, TOK) == whole(col, PAD)) & (part_of(row, TOK) == part_of(col, PAD))
    squeeze = jnp.where(same, 1.0, 0.0).astype(BF16)
    pl.semaphore_wait(barrier, RING - 1 + NY - 1 + 1)

    def own_copy(r):
        return remote(
            stage.at[rem(dp + r, NY)],
            own.at[dp],
            own_sem.at[0, r],
            own_sem.at[1, r],
            {"dp": rem(dp + r, NY)},
        )

    def own_arrival(r):
        source = rem(dp + NY - r, NY)
        return remote(stage.at[source], own.at[source], own_sem.at[0, r], own_sem.at[1, r], {"dp": source})

    for r in range(1, NY):
        own_copy(r).start()
    for r in range(1, NY):
        own_arrival(r).wait_recv()
    own_rows = own[...].reshape(NY * PAD, 2 * width + LANES)
    packed = matmul(squeeze, own_rows).astype(BF16)
    units[half, 0] = packed

    def near(src, dst, toward):
        return remote(
            units.at[half, src],
            units.at[half, dst],
            near_sem.at[0, dst],
            near_sem.at[1, dst],
            {"expert": toward},
        )

    def far(src, dst, toward):
        return remote(
            units.at[half, pl.ds(src * SPAN, SPAN)],
            units.at[half, pl.ds(dst * SPAN, SPAN)],
            far_sem.at[0, dst],
            far_sem.at[1, dst],
            {"expert": toward},
        )

    def near_wait(dst):
        near(dst, dst, z_next).wait_recv()

    def near_pass(src, dst, toward):
        near(src, dst, toward).start()

    def far_wait(dst):
        far(dst, dst, z_next).wait_recv()

    def far_pass(src, dst, toward):
        far(src, dst, toward).start()

    @pl.when(half == 0)
    def _():
        near_pass(0, 1, x_at[3])
        near_pass(0, 3, x_at[1])

    @pl.when(half == 1)
    def _():
        near_pass(0, 1, z_last)
        near_pass(0, 2, z_next)

    def take_first(c):
        @pl.when(c == 0)
        def _():
            near_wait(1)
            near_pass(0, 2, x_at[2])

        @pl.when(c == 1)
        def _():
            near_wait(3)
            near_wait(2)

        @pl.when(c > 1)
        def _():
            far_wait(c)

        @pl.when(c < 2)
        def _():
            far_pass(c, 2 * c + 2, z_last)
            far_pass(c, 2 * c + 3, z_next)

        even = rem(c, 2) == 0

        @pl.when((c > 1) & (c < 11) & even)
        def _():
            far_pass(c, c + 4, z_last)

        @pl.when((c > 1) & (c < 10) & jnp.logical_not(even))
        def _():
            far_pass(c, c + 4, z_next)

        @pl.when(c == 13)
        def _():
            far_pass(c, 15, z_next)

    def take_second(c):
        @pl.when(c == 0)
        def _():
            near_wait(1)
            near_pass(0, 3, z_two_last)
            near_pass(0, 4, z_two_next)

        @pl.when(c == 1)
        def _():
            near_wait(2)
            near_wait(3)
            near_pass(3, 5, z_last)

        @pl.when(c == 2)
        def _():
            near_wait(4)
            near_pass(4, 6, z_next)
            near_wait(5)
            near_pass(5, 7, z_last)

        @pl.when(c == 3)
        def _():
            near_wait(6)
            near_wait(7)

        @pl.when(c > 3)
        def _():
            far_wait(c)

        @pl.when(c < 4)
        def _():
            far_pass(c, 2 * c + 4, x_at[3])
            far_pass(c, 2 * c + 5, x_at[1])

        @pl.when((c == 4) | (c == 6))
        def _():
            far_pass(c, 10 + div(c, 2), x_at[3])

        @pl.when((c == 9) | (c == 11))
        def _():
            far_pass(c, 10 + div(c, 2), x_at[1])

    def take(c):
        pl.when(half == 0)(functools.partial(take_first, c))
        pl.when(half == 1)(functools.partial(take_second, c))
        twin(c, half).start()

    def twin(c, block):
        span = pl.ds(c * SPAN, SPAN)
        return remote(
            units.at[block, span],
            units.at[block, span],
            twin_sem.at[0, c],
            twin_sem.at[1, c],
            {"half": other},
        )

    def sum_copy(stage_no, c, way, src, dst):
        return remote(
            src,
            dst,
            sum_sem.at[stage_no, 0, way, c],
            sum_sem.at[stage_no, 1, way, c],
            {"dp": y_next if way == 0 else y_last},
        )

    def act_copy(stage_no, c, way, view):
        return remote(
            view,
            view,
            act_sem.at[stage_no, 0, way, c],
            act_sem.at[stage_no, 1, way, c],
            {"dp": y_next if way == 0 else y_last},
        )

    def columns(way):
        return pl.ds(way * mid, mid)

    def first_sum(c, way):
        return sum_copy(0, c, way, part.at[c, y_far, :, columns(way)], sum_one.at[c, way])

    def second_sum(c, way):
        toward = y_next if way == 0 else y_last
        return sum_copy(1, c, way, part.at[c, toward], sum_two.at[c, way])

    def select(c):
        chunk = order(c)
        twin(chunk, other).wait_recv()
        span = pl.ds(chunk * SPAN, SPAN)
        stacked = jnp.concatenate(
            [units[b, span].reshape(SPAN * UNIT_TOK, 2 * width + LANES) for b in range(2)], axis=0
        )
        is_expert = lax.broadcasted_iota(jnp.int32, (8, LANES), 1) == expert
        gate_row = matmul(is_expert.astype(BF16), stacked[:, width : width + LANES], 1, 1)
        chosen = gate_row > 0.0
        rank = matmul(chosen.astype(BF16), before_chunk[...])
        token = index_of((8, TOKENS), 1)
        unit = whole(token, UNIT_TOK)
        unit = part_of(unit, SPAN) * 2 + whole(unit, SPAN)
        base = unit * UNIT + part_of(whole(token, TOK), NY) * MOST
        place = jnp.where(chosen, base + rank, -1.0)
        pick = jnp.where(index_of((SLOTS, TOKENS), 0) == place[:1], 1.0, 0.0).astype(BF16)
        gate_wide = matmul(
            pick, jnp.broadcast_to(gate_row[:1], (LANES, TOKENS)).astype(BF16), 1, 1
        )
        gates[c] = gate_wide
        slots = matmul(pick, stacked[:, :width]).astype(BF16)
        slot_x[c] = slots
        slots_d = matmul(pick, stacked[:, width + LANES :])
        slot_s[c] = (gate_wide[:, :1] * slots_d).astype(BF16)
        shape = (NY, PART, hidden)
        part[c, :, :, 0:hidden] = matmul(slots, w_gate[...]).astype(BF16).reshape(shape)
        part[c, :, :, hidden : 2 * hidden] = matmul(slots, w_up[...]).astype(BF16).reshape(shape)
        part[c, :, :, 2 * hidden :] = (
            matmul(slots_d.astype(BF16), w_down[...]).astype(BF16).reshape(shape)
        )
        for way in range(2):
            first_sum(c, way).start()

    def add_passing(c):
        for way in range(2):
            first_sum(c, way).wait_recv()
            toward = y_next if way == 0 else y_last
            here = part[c, toward, :, columns(way)].astype(F32)
            part[c, toward, :, columns(way)] = (here + sum_one[c, way].astype(F32)).astype(BF16)
            second_sum(c, way).start()

    def activate(c):
        for way in range(2):
            second_sum(c, way).wait_recv()
        summed = (
            part[c, dp].astype(F32) + sum_two[c, 0].astype(F32) + sum_two[c, 1].astype(F32)
        )
        gate_act, up_act, back = (
            summed[:, :hidden],
            summed[:, hidden : 2 * hidden],
            summed[:, 2 * hidden :],
        )
        gate_col = gates[c, pl.ds(pl.multiple_of(dp * PART, PART), PART), :][:, :1]
        sigma = jax.nn.sigmoid(gate_act)
        active = gate_act * sigma
        slope = sigma * (1.0 + gate_act * (1.0 - sigma))
        units = (active * up_act).astype(BF16)
        scaled_back = gate_col * back
        act[c, dp, :, 0:hidden] = (scaled_back * up_act * slope).astype(BF16)
        act[c, dp, :, hidden : 2 * hidden] = (scaled_back * active).astype(BF16)
        act[c, dp, :, 2 * hidden :] = units
        route = jnp.sum(back * units.astype(F32), axis=1, keepdims=True)
        gates[c] = jnp.zeros((SLOTS, LANES), F32)
        gates[c, pl.ds(pl.multiple_of(dp * PART, PART), PART), :] = jnp.broadcast_to(
            route, (PART, LANES)
        )
        for way in range(2):
            act_copy(0, c, way, act.at[c, dp]).start()

    def pass_act(c):
        for way in range(2):
            source = y_last if way == 0 else y_next
            act_copy(0, c, way, act.at[c, source]).wait_recv()
            act_copy(1, c, way, act.at[c, source, :, columns(way)]).start()

    def half_copy(c):
        return remote(
            row_part.at[c, :, other],
            row_other.at[c],
            half_sem.at[0, c],
            half_sem.at[1, c],
            {"half": other},
        )

    def row_terms(c):
        for way in range(2):
            act_copy(1, c, way, act.at[c, y_far, :, columns(way)]).wait_recv()
        grads = act[c].reshape(SLOTS, three)
        rows = matmul(grads[:, :hidden], w_gate[...], 1, 1) + matmul(
            grads[:, hidden : 2 * hidden], w_up[...], 1, 1
        )
        row_part[c, :, :, :, 0:width] = rows.astype(BF16).reshape(SPAN, 2, UNIT, width)
        row_part[c, :, :, :, width:] = gates[c].astype(BF16).reshape(SPAN, 2, UNIT, LANES)
        half_copy(c).start()

    def back_copy(place, c, j, toward):
        return remote(
            row_send.at[c, j],
            row_back.at[expert],
            back_send.at[place],
            back_recv.at[expert],
            {"expert": toward},
        )

    def give_back(c):
        half_copy(c).wait_recv()
        for j in range(SPAN):
            place = c * SPAN + j
            row_send[c, j] = (
                row_part[c, j, half].astype(F32) + row_other[c, j].astype(F32)
            ).astype(BF16)
            toward = owner(expert, half, order(c), j)

            @pl.when(place != 0)
            def _():
                back_copy(place, c, j, toward).start()

            @pl.when(place == 0)
            def _():
                row_back[expert] = row_send[c, j]

    def weight_terms(c):
        pair = pl.ds(c - 1, 2)

        def tile(m, carry):
            span = pl.ds(pl.multiple_of(m * LANES, LANES), LANES)
            acc[span, : 2 * hidden] += matmul(
                slot_x[pair, :, span].reshape(2 * SLOTS, LANES),
                act[pair, :, :, : 2 * hidden].reshape(2 * SLOTS, 2 * hidden),
                0,
                0,
            )
            acc[span, 2 * hidden :] += matmul(
                slot_s[pair, :, span].reshape(2 * SLOTS, LANES),
                act[pair, :, :, 2 * hidden :].reshape(2 * SLOTS, hidden),
                0,
                0,
            )
            return carry

        @pl.when(rem(c, 2) == 1)
        def _():
            lax.fori_loop(0, width // LANES, tile, 0)

    for load in loads:
        load.wait()

    def sent(c):
        twin(c, half).wait_send()
        for way in range(2):
            first_sum(c, way).wait_send()
            second_sum(c, way).wait_send()
            act_copy(0, c, way, act.at[c, dp]).wait_send()
            act_copy(1, c, way, act.at[c, y_far, :, columns(way)]).wait_send()
        half_copy(c).wait_send()

        @pl.when(c == 0)
        def _():
            for dst in range(1, NX):
                near(0, dst, z_next).wait_send()

        @pl.when((c == 0) & (half == 1))
        def _():
            for dst in range(NX, NZ):
                near(0, dst, z_next).wait_send()

        @pl.when((c > 3) | ((c > 1) & (half == 0)))
        def _():
            far(0, c, z_next).wait_send()

        @pl.when(c == 2)
        def _():
            back_copy(1, 0, 0, z_next).wait_send()

        @pl.when(c > 2)
        def _():
            for j in range(SPAN):
                back_copy((c - 2) * SPAN + j, 0, 0, z_next).wait_send()

    def turn(i, carry):
        def staged(lag, work):
            pl.when((i >= lag) & (i - lag < CHUNKS))(functools.partial(work, i - lag))

        staged(7, pass_act)
        staged(5, activate)
        staged(3, add_passing)
        staged(1, select)
        first = i + jnp.where(i > 4, 1, 0)
        beyond = jnp.minimum(i + 1 + jnp.where(i > 3, 1, 0), CHUNKS)

        def take_one(c, carry):
            take(c)
            return carry

        lax.fori_loop(first, beyond, take_one, 0)
        staged(9, row_terms)
        staged(10, give_back)
        staged(11, weight_terms)
        staged(11, sent)
        return carry

    lax.fori_loop(0, CHUNKS + 11, turn, 0)

    stores = []
    for n in range(3):
        grads_out[n] = acc[:, n * hidden : (n + 1) * hidden].astype(BF16)
        stores.append(pltpu.make_async_copy(grads_out.at[n], grads_hbm.at[n], load_sem.at[3 + n]))
        stores[n].start()

    own_gate = own_rows[:, width : width + LANES]
    own_chosen = (own_gate.astype(F32) > 0.0).astype(BF16)
    own_rank = matmul(before(NY * PAD, PAD), own_chosen, 0, 0).astype(BF16)
    returns = RING * UNIT
    spread = jnp.where(
        index_of((LANES, returns), 0) == whole(index_of((LANES, returns), 1), UNIT), 1.0, 0.0
    ).astype(BF16)
    chosen_at = matmul(own_chosen, spread)
    rank_at = matmul(own_rank, spread)
    own_token, slot = index_of((NY * PAD, returns), 0), index_of((NY * PAD, returns), 1)
    fits = (rank_at == part_of(slot, MOST)) & (
        whole(own_token, PAD) == part_of(whole(slot, MOST), NY)
    )
    combine = jnp.where(fits, chosen_at, 0.0).astype(BF16)
    gather = jnp.where(
        whole(index_of((returns, LANES), 0), UNIT) == index_of((returns, LANES), 1), 1.0, 0.0
    ).astype(BF16)

    def arrival(i, carry):
        source = rem(expert + i, RING)
        remote(
            row_send.at[0, 0],
            row_back.at[source],
            back_send.at[0],
            back_recv.at[source],
            {"expert": source},
        ).wait_recv()
        return carry

    lax.fori_loop(1, RING, arrival, 0)
    returned = row_back[...].reshape(RING * UNIT, width + LANES)
    token_sum = matmul(combine, returned[:, :width])
    route_sum = matmul(combine, returned[:, width:] * gather)
    fin_send[:, :, 0:width] = token_sum.astype(BF16).reshape(NY, PAD, width)
    fin_send[:, :, width:] = route_sum.astype(BF16).reshape(NY, PAD, LANES)

    def fin_copy(r):
        return remote(
            fin_send.at[rem(dp + r, NY)],
            fin_recv.at[dp],
            fin_sem.at[0, r],
            fin_sem.at[1, r],
            {"dp": rem(dp + r, NY)},
        )

    def fin_arrival(r):
        source = rem(dp + NY - r, NY)
        return remote(
            fin_send.at[source], fin_recv.at[source], fin_sem.at[0, r], fin_sem.at[1, r], {"dp": source}
        )

    for r in range(1, NY):
        fin_copy(r).start()
    fin_recv[dp] = fin_send[dp]
    for r in range(1, NY):
        fin_arrival(r).wait_recv()
    routes = jnp.zeros((PAD, LANES), F32)
    for q in range(NY):
        token_out[:, q * width : (q + 1) * width] = fin_recv[q, :, 0:width]
        routes = routes + fin_recv[q, :, width:].astype(F32)
    unit = jnp.where(index_of((LANES, LANES), 0) == index_of((LANES, LANES), 1), 1.0, 0.0)
    by_expert = matmul(unit.astype(BF16), routes.astype(BF16), 1, 1)[:, :TOK]
    lane = lax.broadcasted_iota(jnp.int32, (LANES, TOK), 0)
    named = ids[half]
    for k in range(TOP):
        value = jnp.where(named[k : k + 1] == lane, by_expert, 0.0)
        route_out[k : k + 1] = jnp.sum(value, axis=0, keepdims=True)
    for store in stores:
        store.wait()
    for r in range(1, NY):
        own_copy(r).wait_send()
        fin_copy(r).wait_send()

    for place in range((CHUNKS - 2) * SPAN, RING):
        back_copy(place, 0, 0, z_next).wait_send()


def finish(token_rows, route_rows, grads, token_out, route_out, gate_out, up_out, down_out, held, sem):
    targets = (gate_out, up_out, down_out)
    loads = [pltpu.make_async_copy(grads.at[n], held.at[n], sem.at[0, n]) for n in range(3)]
    stores = [pltpu.make_async_copy(held.at[n], targets[n].at[0], sem.at[1, n]) for n in range(3)]
    for load in loads:
        load.start()
    token_out[0, 0] = token_rows[:TOK]
    route_out[0, 0] = route_rows[...].astype(BF16)
    for load, store in zip(loads, stores):
        load.wait()
        store.start()
    for store in stores:
        store.wait()


def on_device(tokens_in, cotangent, expert_ids, gate_probs, gate_weight, up_weight, down_weight):
    width, hidden = gate_weight.shape[1], gate_weight.shape[2]
    three = 3 * hidden
    vmem = pl.BlockSpec(memory_space=pltpu.VMEM)
    hbm = pl.BlockSpec(memory_space=pl.ANY)
    out = pl.pallas_call(
        functools.partial(kernel, width, hidden),
        out_shape=(
            jax.ShapeDtypeStruct((PAD, NY * width), BF16),
            jax.ShapeDtypeStruct((TOP, TOK), F32),
            jax.ShapeDtypeStruct((3, width, hidden), BF16),
        ),
        in_specs=[vmem] * 4 + [hbm] * 3,
        out_specs=(vmem, vmem, hbm),
        scratch_shapes=[
            *[pltpu.VMEM((width, hidden), BF16)] * 3,
            pltpu.VMEM((TOKENS, TOKENS), BF16),
            *[pltpu.VMEM((NY, PAD, 2 * width + LANES), BF16)] * 2,
            pltpu.VMEM((2, RING, UNIT_TOK, 2 * width + LANES), BF16),
            pltpu.VMEM((CHUNKS, SLOTS, width), BF16),
            pltpu.VMEM((CHUNKS, SLOTS, width), BF16),
            pltpu.VMEM((CHUNKS, SLOTS, LANES), F32),
            pltpu.VMEM((CHUNKS, NY, PART, three), BF16),
            pltpu.VMEM((CHUNKS, 2, PART, three // 2), BF16),
            pltpu.VMEM((CHUNKS, 2, PART, three), BF16),
            pltpu.VMEM((CHUNKS, NY, PART, three), BF16),
            pltpu.VMEM((CHUNKS, SPAN, 2, UNIT, width + LANES), BF16),
            pltpu.VMEM((CHUNKS, SPAN, UNIT, width + LANES), BF16),
            pltpu.VMEM((CHUNKS, SPAN, UNIT, width + LANES), BF16),
            pltpu.VMEM((RING, UNIT, width + LANES), BF16),
            pltpu.VMEM((NY, PAD, width + LANES), BF16),
            pltpu.VMEM((NY, PAD, width + LANES), BF16),
            pltpu.VMEM((width, three), F32),
            pltpu.VMEM((3, width, hidden), BF16),
            pltpu.SemaphoreType.DMA((2, NY)),
            pltpu.SemaphoreType.DMA((2, NZ)),
            pltpu.SemaphoreType.DMA((2, CHUNKS)),
            pltpu.SemaphoreType.DMA((2, CHUNKS)),
            pltpu.SemaphoreType.DMA((2, 2, 2, CHUNKS)),
            pltpu.SemaphoreType.DMA((2, 2, 2, CHUNKS)),
            pltpu.SemaphoreType.DMA((2, CHUNKS)),
            pltpu.SemaphoreType.DMA((RING,)),
            pltpu.SemaphoreType.DMA((RING,)),
            pltpu.SemaphoreType.DMA((2, NY)),
            pltpu.SemaphoreType.DMA((6,)),
        ],
        compiler_params=pltpu.CompilerParams(
            collective_id=0, has_side_effects=True, vmem_limit_bytes=62 * 1024 * 1024
        ),
    )(
        tokens_in[0].transpose(1, 0, 2),
        cotangent[0].transpose(1, 0, 2),
        expert_ids[0].transpose(0, 2, 1),
        gate_probs[0].transpose(0, 2, 1),
        gate_weight[0],
        up_weight[0],
        down_weight[0],
    )
    weights = jax.ShapeDtypeStruct((1, width, hidden), BF16)
    token_grad, route_grad, *grads = pl.pallas_call(
        finish,
        out_shape=(
            jax.ShapeDtypeStruct((1, 1, TOK, NY * width), BF16),
            jax.ShapeDtypeStruct((1, 1, TOP, TOK), BF16),
            weights,
            weights,
            weights,
        ),
        in_specs=[vmem, vmem, hbm],
        out_specs=(vmem, vmem, hbm, hbm, hbm),
        scratch_shapes=[pltpu.VMEM((3, width, hidden), BF16), pltpu.SemaphoreType.DMA((2, 3))],
    )(*out)
    return token_grad, route_grad.transpose(0, 1, 3, 2), *grads


def solution(mesh):
    return jax.shard_map(
        on_device,
        mesh=mesh,
        in_specs=(
            P(("expert", "dp"), None, None, None),
            P(("expert", "dp"), None, None, None),
            P(("expert", "dp"), None, None, None),
            P(("expert", "dp"), None, None, None),
            P("expert", "dp", "half"),
            P("expert", "dp", "half"),
            P("expert", "dp", "half"),
        ),
        out_specs=(
            P(("expert", "dp"), "half", None, None),
            P(("expert", "dp"), "half", None, None),
            P("expert", "dp", "half"),
            P("expert", "dp", "half"),
            P("expert", "dp", "half"),
        ),
        check_vma=False,
    )
```

```python
import functools

import jax
import jax.numpy as jnp
from jax import lax
from jax.experimental import pallas as pl
from jax.experimental.pallas import tpu as pltpu
from jax.sharding import PartitionSpec as P

MESH = pl.DeviceIdType.MESH
BF16 = jnp.bfloat16
F32 = jnp.float32

TOP = 8
MOST = 6
TOK = 12
PAD = 16
NX, NY, NZ = 4, 4, 8
RING = NX * NZ
LAST = NZ // 2
SPAN = 2
CHUNKS = RING // SPAN
UNIT_TOK = NY * TOK
UNIT = NY * MOST
TOKENS = 2 * SPAN * UNIT_TOK
SLOTS = 2 * SPAN * UNIT
PART = SLOTS // NY
LANES = 128


def rem(a, b):
    return lax.rem(a, jnp.int32(b))


def div(a, b):
    return lax.div(a, jnp.int32(b))


def choose(index, values):
    found = jnp.int32(values[0])
    for i, value in enumerate(values[1:], 1):
        if value != values[0]:
            found = jnp.where(index == i, jnp.int32(value), found)
    return found


Z_ORDER = (0, 1, 7, 2, 6, 3, 5, 4)
FIRST_Z = (0, 0, 1, 7, 1, 7, 2, 6, 2, 6, 3, 5, 3, 5, 4, 4)
FIRST_X = (0, 1, 0, 0, 1, 1, 0, 0, 1, 1, 0, 0, 1, 1, 0, 1)
SECOND_X = (0, 0, 0, 0, 1, 3, 1, 3, 1, 3, 1, 3, 2, 2, 2, 2)
SECOND_Z = (0, 1, 2, 3, 0, 0, 1, 1, 2, 2, 3, 3, 0, 1, 2, 3)


def order(n):
    return jnp.where(n < 4, n, jnp.where(n == CHUNKS - 1, 4, n + 1))


def owner(expert, half, c, j):
    x, z = div(expert, NZ), rem(expert, NZ)
    first = rem(x + choose(c, FIRST_X) * SPAN + j, NX) * NZ + rem(z + choose(c, FIRST_Z), NZ)
    z_step = choose(choose(c, SECOND_Z) * SPAN + j, Z_ORDER)
    second = rem(x + choose(c, SECOND_X), NX) * NZ + rem(z + z_step, NZ)
    return first + half * (second - first)


def index_of(shape, dim):
    return lax.broadcasted_iota(jnp.int32, shape, dim).astype(F32)


def whole(number, size):
    return jnp.floor((number + 0.5) * (1.0 / size))


def part_of(number, size):
    return number - size * whole(number, size)


def before(size, span):
    row, col = index_of((size, size), 0), index_of((size, size), 1)
    return jnp.where((whole(row, span) == whole(col, span)) & (row < col), 1.0, 0.0).astype(BF16)


def matmul(a, b, a_dim=1, b_dim=0):
    return lax.dot_general(a, b, (((a_dim,), (b_dim,)), ((), ())), preferred_element_type=F32)


def kernel(
    width,
    hidden,
    tokens,
    cotangent,
    ids,
    probs,
    w_gate_hbm,
    w_up_hbm,
    w_down_hbm,
    token_out,
    route_out,
    grads_hbm,
    w_gate,
    w_up,
    w_down,
    before_chunk,
    stage,
    own,
    units,
    slot_x,
    slot_s,
    gates,
    part,
    sum_one,
    sum_two,
    act,
    row_part,
    row_other,
    row_send,
    row_back,
    fin_send,
    fin_recv,
    acc,
    grads_out,
    own_sem,
    near_sem,
    far_sem,
    twin_sem,
    sum_sem,
    act_sem,
    half_sem,
    back_send,
    back_recv,
    fin_sem,
    load_sem,
):
    loads = [
        pltpu.make_async_copy(src, dst, load_sem.at[n])
        for n, (src, dst) in enumerate(((w_gate_hbm, w_gate), (w_up_hbm, w_up), (w_down_hbm, w_down)))
    ]
    for load in loads:
        load.start()
    expert, half, dp = lax.axis_index("expert"), lax.axis_index("half"), lax.axis_index("dp")
    other = 1 - half
    x, z = div(expert, NZ), rem(expert, NZ)
    z_next, z_last = x * NZ + rem(z + 1, NZ), x * NZ + rem(z + NZ - 1, NZ)
    z_two_next, z_two_last = x * NZ + rem(z + 2, NZ), x * NZ + rem(z + NZ - 2, NZ)
    x_at = [rem(x + r, NX) * NZ + z for r in range(NX)]
    y_next, y_last, y_far = rem(dp + 1, NY), rem(dp + 3, NY), rem(dp + 2, NY)
    three = 3 * hidden
    mid = three // 2

    def remote(src, dst, send, recv, where):
        return pltpu.make_async_remote_copy(
            src_ref=src, dst_ref=dst, send_sem=send, recv_sem=recv, device_id=where, device_id_type=MESH
        )

    barrier = pltpu.get_barrier_semaphore()

    def greet(i, carry):
        pl.semaphore_signal(
            barrier, inc=1, device_id={"expert": rem(expert + i, RING)}, device_id_type=MESH
        )
        return carry

    lax.fori_loop(1, RING, greet, 0)
    for r in range(1, NY):
        pl.semaphore_signal(barrier, inc=1, device_id={"dp": rem(dp + r, NY)}, device_id_type=MESH)
    pl.semaphore_signal(barrier, inc=1, device_id={"half": other}, device_id_type=MESH)
    acc[...] = jnp.zeros_like(acc)
    before_chunk[...] = before(TOKENS, TOK)
    row, col = index_of((PAD, 2 * TOK), 0), index_of((PAD, 2 * TOK), 1)
    mine = jnp.where((row < TOK) & (col == 2 * row + half), 1.0, 0.0).astype(BF16)
    block_x = matmul(mine, tokens[...].reshape(2 * TOK, NY * width)).astype(BF16)
    block_d = matmul(mine, cotangent[...].reshape(2 * TOK, NY * width)).astype(BF16)
    named, weight = ids[half], probs[half].astype(F32)
    lane = lax.broadcasted_iota(jnp.int32, (LANES, TOK), 0)
    gate_map = jnp.zeros((LANES, TOK), F32)
    for k in range(TOP):
        gate_map = jnp.where(named[k : k + 1] == lane, weight[k : k + 1], gate_map)
    unit = jnp.where(index_of((PAD, TOK), 0) == index_of((PAD, TOK), 1), 1.0, 0.0).astype(BF16)
    gate_map = matmul(unit, gate_map.astype(BF16), 1, 1).astype(BF16)
    for q in range(NY):
        stage[q, :, 0:width] = block_x[:, q * width : (q + 1) * width]
        stage[q, :, width : width + LANES] = gate_map
        stage[q, :, width + LANES :] = block_d[:, q * width : (q + 1) * width]
    own[dp] = stage[dp]
    row, col = index_of((UNIT_TOK, NY * PAD), 0), index_of((UNIT_TOK, NY * PAD), 1)
    same = (whole(row, TOK) == whole(col, PAD)) & (part_of(row, TOK) == part_of(col, PAD))
    squeeze = jnp.where(same, 1.0, 0.0).astype(BF16)
    pl.semaphore_wait(barrier, RING - 1 + NY - 1 + 1)

    def own_copy(r):
        return remote(
            stage.at[rem(dp + r, NY)],
            own.at[dp],
            own_sem.at[0, r],
            own_sem.at[1, r],
            {"dp": rem(dp + r, NY)},
        )

    def own_arrival(r):
        source = rem(dp + NY - r, NY)
        return remote(stage.at[source], own.at[source], own_sem.at[0, r], own_sem.at[1, r], {"dp": source})

    for r in range(1, NY):
        own_copy(r).start()
    for r in range(1, NY):
        own_arrival(r).wait_recv()
    own_rows = own[...].reshape(NY * PAD, 2 * width + LANES)
    packed = matmul(squeeze, own_rows).astype(BF16)
    units[half, 0] = packed

    def near(src, dst, toward):
        return remote(
            units.at[half, src],
            units.at[half, dst],
            near_sem.at[0, dst],
            near_sem.at[1, dst],
            {"expert": toward},
        )

    def far(src, dst, toward):
        return remote(
            units.at[half, pl.ds(src * SPAN, SPAN)],
            units.at[half, pl.ds(dst * SPAN, SPAN)],
            far_sem.at[0, dst],
            far_sem.at[1, dst],
            {"expert": toward},
        )

    def near_wait(dst):
        near(dst, dst, z_next).wait_recv()

    def near_pass(src, dst, toward):
        near(src, dst, toward).start()

    def far_wait(dst):
        far(dst, dst, z_next).wait_recv()

    def far_pass(src, dst, toward):
        far(src, dst, toward).start()

    @pl.when(half == 0)
    def _():
        near_pass(0, 1, x_at[3])
        near_pass(0, 3, x_at[1])

    @pl.when(half == 1)
    def _():
        near_pass(0, 1, z_last)
        near_pass(0, 2, z_next)

    def take_first(c):
        @pl.when(c == 0)
        def _():
            near_wait(1)
            near_pass(0, 2, x_at[2])

        @pl.when(c == 1)
        def _():
            near_wait(3)
            near_wait(2)

        @pl.when(c > 1)
        def _():
            far_wait(c)

        @pl.when(c < 2)
        def _():
            far_pass(c, 2 * c + 2, z_last)
            far_pass(c, 2 * c + 3, z_next)

        even = rem(c, 2) == 0

        @pl.when((c > 1) & (c < 11) & even)
        def _():
            far_pass(c, c + 4, z_last)

        @pl.when((c > 1) & (c < 10) & jnp.logical_not(even))
        def _():
            far_pass(c, c + 4, z_next)

        @pl.when(c == 13)
        def _():
            far_pass(c, 15, z_next)

    def take_second(c):
        @pl.when(c == 0)
        def _():
            near_wait(1)
            near_pass(0, 3, z_two_last)
            near_pass(0, 4, z_two_next)

        @pl.when(c == 1)
        def _():
            near_wait(2)
            near_wait(3)
            near_pass(3, 5, z_last)

        @pl.when(c == 2)
        def _():
            near_wait(4)
            near_pass(4, 6, z_next)
            near_wait(5)
            near_pass(5, 7, z_last)

        @pl.when(c == 3)
        def _():
            near_wait(6)
            near_wait(7)

        @pl.when(c > 3)
        def _():
            far_wait(c)

        @pl.when(c < 4)
        def _():
            far_pass(c, 2 * c + 4, x_at[3])
            far_pass(c, 2 * c + 5, x_at[1])

        @pl.when((c == 4) | (c == 6))
        def _():
            far_pass(c, 10 + div(c, 2), x_at[3])

        @pl.when((c == 9) | (c == 11))
        def _():
            far_pass(c, 10 + div(c, 2), x_at[1])

    def take(c):
        pl.when(half == 0)(functools.partial(take_first, c))
        pl.when(half == 1)(functools.partial(take_second, c))
        twin(c, half).start()

    def twin(c, block):
        span = pl.ds(c * SPAN, SPAN)
        return remote(
            units.at[block, span],
            units.at[block, span],
            twin_sem.at[0, c],
            twin_sem.at[1, c],
            {"half": other},
        )

    def sum_copy(stage_no, c, way, src, dst):
        return remote(
            src,
            dst,
            sum_sem.at[stage_no, 0, way, c],
            sum_sem.at[stage_no, 1, way, c],
            {"dp": y_next if way == 0 else y_last},
        )

    def act_copy(stage_no, c, way, view):
        return remote(
            view,
            view,
            act_sem.at[stage_no, 0, way, c],
            act_sem.at[stage_no, 1, way, c],
            {"dp": y_next if way == 0 else y_last},
        )

    def columns(way):
        return pl.ds(way * mid, mid)

    def first_sum(c, way):
        return sum_copy(0, c, way, part.at[c, y_far, :, columns(way)], sum_one.at[c, way])

    def second_sum(c, way):
        toward = y_next if way == 0 else y_last
        return sum_copy(1, c, way, part.at[c, toward], sum_two.at[c, way])

    def select(c):
        chunk = order(c)
        twin(chunk, other).wait_recv()
        span = pl.ds(chunk * SPAN, SPAN)
        stacked = jnp.concatenate(
            [units[b, span].reshape(SPAN * UNIT_TOK, 2 * width + LANES) for b in range(2)], axis=0
        )
        is_expert = lax.broadcasted_iota(jnp.int32, (8, LANES), 1) == expert
        gate_row = matmul(is_expert.astype(BF16), stacked[:, width : width + LANES], 1, 1)
        chosen = gate_row > 0.0
        rank = matmul(chosen.astype(BF16), before_chunk[...])
        token = index_of((8, TOKENS), 1)
        unit = whole(token, UNIT_TOK)
        unit = part_of(unit, SPAN) * 2 + whole(unit, SPAN)
        base = unit * UNIT + part_of(whole(token, TOK), NY) * MOST
        place = jnp.where(chosen, base + rank, -1.0)
        pick = jnp.where(index_of((SLOTS, TOKENS), 0) == place[:1], 1.0, 0.0).astype(BF16)
        gate_wide = matmul(
            pick, jnp.broadcast_to(gate_row[:1], (LANES, TOKENS)).astype(BF16), 1, 1
        )
        gates[c] = gate_wide
        slots = matmul(pick, stacked[:, :width]).astype(BF16)
        slot_x[c] = slots
        slots_d = matmul(pick, stacked[:, width + LANES :])
        slot_s[c] = (gate_wide[:, :1] * slots_d).astype(BF16)
        shape = (NY, PART, hidden)
        part[c, :, :, 0:hidden] = matmul(slots, w_gate[...]).astype(BF16).reshape(shape)
        part[c, :, :, hidden : 2 * hidden] = matmul(slots, w_up[...]).astype(BF16).reshape(shape)
        part[c, :, :, 2 * hidden :] = (
            matmul(slots_d.astype(BF16), w_down[...]).astype(BF16).reshape(shape)
        )
        for way in range(2):
            first_sum(c, way).start()

    def add_passing(c):
        for way in range(2):
            first_sum(c, way).wait_recv()
            toward = y_next if way == 0 else y_last
            here = part[c, toward, :, columns(way)].astype(F32)
            part[c, toward, :, columns(way)] = (here + sum_one[c, way].astype(F32)).astype(BF16)
            second_sum(c, way).start()

    def activate(c):
        for way in range(2):
            second_sum(c, way).wait_recv()
        summed = (
            part[c, dp].astype(F32) + sum_two[c, 0].astype(F32) + sum_two[c, 1].astype(F32)
        )
        gate_act, up_act, back = (
            summed[:, :hidden],
            summed[:, hidden : 2 * hidden],
            summed[:, 2 * hidden :],
        )
        gate_col = gates[c, pl.ds(pl.multiple_of(dp * PART, PART), PART), :][:, :1]
        sigma = jax.nn.sigmoid(gate_act)
        active = gate_act * sigma
        slope = sigma * (1.0 + gate_act * (1.0 - sigma))
        units = (active * up_act).astype(BF16)
        scaled_back = gate_col * back
        act[c, dp, :, 0:hidden] = (scaled_back * up_act * slope).astype(BF16)
        act[c, dp, :, hidden : 2 * hidden] = (scaled_back * active).astype(BF16)
        act[c, dp, :, 2 * hidden :] = units
        route = jnp.sum(back * units.astype(F32), axis=1, keepdims=True)
        gates[c] = jnp.zeros((SLOTS, LANES), F32)
        gates[c, pl.ds(pl.multiple_of(dp * PART, PART), PART), :] = jnp.broadcast_to(
            route, (PART, LANES)
        )
        for way in range(2):
            act_copy(0, c, way, act.at[c, dp]).start()

    def pass_act(c):
        for way in range(2):
            source = y_last if way == 0 else y_next
            act_copy(0, c, way, act.at[c, source]).wait_recv()
            act_copy(1, c, way, act.at[c, source, :, columns(way)]).start()

    def half_copy(c):
        return remote(
            row_part.at[c, :, other],
            row_other.at[c],
            half_sem.at[0, c],
            half_sem.at[1, c],
            {"half": other},
        )

    def row_terms(c):
        for way in range(2):
            act_copy(1, c, way, act.at[c, y_far, :, columns(way)]).wait_recv()
        grads = act[c].reshape(SLOTS, three)
        rows = matmul(grads[:, :hidden], w_gate[...], 1, 1) + matmul(
            grads[:, hidden : 2 * hidden], w_up[...], 1, 1
        )
        row_part[c, :, :, :, 0:width] = rows.astype(BF16).reshape(SPAN, 2, UNIT, width)
        row_part[c, :, :, :, width:] = gates[c].astype(BF16).reshape(SPAN, 2, UNIT, LANES)
        half_copy(c).start()

    def back_copy(place, c, j, toward):
        return remote(
            row_send.at[c, j],
            row_back.at[expert],
            back_send.at[place],
            back_recv.at[expert],
            {"expert": toward},
        )

    def give_back(c):
        half_copy(c).wait_recv()
        for j in range(SPAN):
            place = c * SPAN + j
            row_send[c, j] = (
                row_part[c, j, half].astype(F32) + row_other[c, j].astype(F32)
            ).astype(BF16)
            toward = owner(expert, half, order(c), j)

            @pl.when(place != 0)
            def _():
                back_copy(place, c, j, toward).start()

            @pl.when(place == 0)
            def _():
                row_back[expert] = row_send[c, j]

    def weight_terms(c):
        pair = pl.ds(c - 1, 2)

        def tile(m, carry):
            span = pl.ds(pl.multiple_of(m * LANES, LANES), LANES)
            acc[span, : 2 * hidden] += matmul(
                slot_x[pair, :, span].reshape(2 * SLOTS, LANES),
                act[pair, :, :, : 2 * hidden].reshape(2 * SLOTS, 2 * hidden),
                0,
                0,
            )
            acc[span, 2 * hidden :] += matmul(
                slot_s[pair, :, span].reshape(2 * SLOTS, LANES),
                act[pair, :, :, 2 * hidden :].reshape(2 * SLOTS, hidden),
                0,
                0,
            )
            return carry

        @pl.when(rem(c, 2) == 1)
        def _():
            lax.fori_loop(0, width // LANES, tile, 0)

    for load in loads:
        load.wait()

    def sent(c):
        twin(c, half).wait_send()
        for way in range(2):
            first_sum(c, way).wait_send()
            second_sum(c, way).wait_send()
            act_copy(0, c, way, act.at[c, dp]).wait_send()
            act_copy(1, c, way, act.at[c, y_far, :, columns(way)]).wait_send()
        half_copy(c).wait_send()

        @pl.when(c == 0)
        def _():
            for dst in range(1, NX):
                near(0, dst, z_next).wait_send()

        @pl.when((c == 0) & (half == 1))
        def _():
            for dst in range(NX, NZ):
                near(0, dst, z_next).wait_send()

        @pl.when((c > 3) | ((c > 1) & (half == 0)))
        def _():
            far(0, c, z_next).wait_send()

        @pl.when(c == 2)
        def _():
            back_copy(1, 0, 0, z_next).wait_send()

        @pl.when(c > 2)
        def _():
            for j in range(SPAN):
                back_copy((c - 2) * SPAN + j, 0, 0, z_next).wait_send()

    def turn(i, carry):
        def staged(lag, work):
            pl.when((i >= lag) & (i - lag < CHUNKS))(functools.partial(work, i - lag))

        staged(7, pass_act)
        staged(5, activate)
        staged(3, add_passing)
        staged(8, row_terms)
        staged(1, select)
        first = i + jnp.where(i > 4, 1, 0)
        beyond = jnp.minimum(i + 1 + jnp.where(i > 3, 1, 0), CHUNKS)

        def take_one(c, carry):
            take(c)
            return carry

        lax.fori_loop(first, beyond, take_one, 0)
        staged(8, give_back)
        staged(9, weight_terms)
        staged(10, sent)
        return carry

    lax.fori_loop(0, CHUNKS + 10, turn, 0)

    stores = []
    for n in range(3):
        grads_out[n] = acc[:, n * hidden : (n + 1) * hidden].astype(BF16)
        stores.append(pltpu.make_async_copy(grads_out.at[n], grads_hbm.at[n], load_sem.at[3 + n]))
        stores[n].start()

    own_gate = own_rows[:, width : width + LANES]
    own_chosen = (own_gate.astype(F32) > 0.0).astype(BF16)
    own_rank = matmul(before(NY * PAD, PAD), own_chosen, 0, 0).astype(BF16)
    returns = RING * UNIT
    spread = jnp.where(
        index_of((LANES, returns), 0) == whole(index_of((LANES, returns), 1), UNIT), 1.0, 0.0
    ).astype(BF16)
    chosen_at = matmul(own_chosen, spread)
    rank_at = matmul(own_rank, spread)
    own_token, slot = index_of((NY * PAD, returns), 0), index_of((NY * PAD, returns), 1)
    fits = (rank_at == part_of(slot, MOST)) & (
        whole(own_token, PAD) == part_of(whole(slot, MOST), NY)
    )
    combine = jnp.where(fits, chosen_at, 0.0).astype(BF16)
    gather = jnp.where(
        whole(index_of((returns, LANES), 0), UNIT) == index_of((returns, LANES), 1), 1.0, 0.0
    ).astype(BF16)

    def arrival(i, carry):
        source = rem(expert + i, RING)
        remote(
            row_send.at[0, 0],
            row_back.at[source],
            back_send.at[0],
            back_recv.at[source],
            {"expert": source},
        ).wait_recv()
        return carry

    lax.fori_loop(1, RING, arrival, 0)
    returned = row_back[...].reshape(RING * UNIT, width + LANES)
    token_sum = matmul(combine, returned[:, :width])
    route_sum = matmul(combine, returned[:, width:] * gather)
    fin_send[:, :, 0:width] = token_sum.astype(BF16).reshape(NY, PAD, width)
    fin_send[:, :, width:] = route_sum.astype(BF16).reshape(NY, PAD, LANES)

    def fin_copy(r):
        return remote(
            fin_send.at[rem(dp + r, NY)],
            fin_recv.at[dp],
            fin_sem.at[0, r],
            fin_sem.at[1, r],
            {"dp": rem(dp + r, NY)},
        )

    def fin_arrival(r):
        source = rem(dp + NY - r, NY)
        return remote(
            fin_send.at[source], fin_recv.at[source], fin_sem.at[0, r], fin_sem.at[1, r], {"dp": source}
        )

    for r in range(1, NY):
        fin_copy(r).start()
    fin_recv[dp] = fin_send[dp]
    for r in range(1, NY):
        fin_arrival(r).wait_recv()
    routes = jnp.zeros((PAD, LANES), F32)
    for q in range(NY):
        token_out[:, q * width : (q + 1) * width] = fin_recv[q, :, 0:width]
        routes = routes + fin_recv[q, :, width:].astype(F32)
    unit = jnp.where(index_of((LANES, LANES), 0) == index_of((LANES, LANES), 1), 1.0, 0.0)
    by_expert = matmul(unit.astype(BF16), routes.astype(BF16), 1, 1)[:, :TOK]
    lane = lax.broadcasted_iota(jnp.int32, (LANES, TOK), 0)
    named = ids[half]
    for k in range(TOP):
        value = jnp.where(named[k : k + 1] == lane, by_expert, 0.0)
        route_out[k : k + 1] = jnp.sum(value, axis=0, keepdims=True)
    for store in stores:
        store.wait()
    for r in range(1, NY):
        own_copy(r).wait_send()
        fin_copy(r).wait_send()

    for place in range((CHUNKS - 2) * SPAN, RING):
        back_copy(place, 0, 0, z_next).wait_send()


def finish(token_rows, route_rows, grads, token_out, route_out, gate_out, up_out, down_out, held, sem):
    targets = (gate_out, up_out, down_out)
    loads = [pltpu.make_async_copy(grads.at[n], held.at[n], sem.at[0, n]) for n in range(3)]
    stores = [pltpu.make_async_copy(held.at[n], targets[n].at[0], sem.at[1, n]) for n in range(3)]
    for load in loads:
        load.start()
    token_out[0, 0] = token_rows[:TOK]
    route_out[0, 0] = route_rows[...].astype(BF16)
    for load, store in zip(loads, stores):
        load.wait()
        store.start()
    for store in stores:
        store.wait()


def on_device(tokens_in, cotangent, expert_ids, gate_probs, gate_weight, up_weight, down_weight):
    width, hidden = gate_weight.shape[1], gate_weight.shape[2]
    three = 3 * hidden
    vmem = pl.BlockSpec(memory_space=pltpu.VMEM)
    hbm = pl.BlockSpec(memory_space=pl.ANY)
    out = pl.pallas_call(
        functools.partial(kernel, width, hidden),
        out_shape=(
            jax.ShapeDtypeStruct((PAD, NY * width), BF16),
            jax.ShapeDtypeStruct((TOP, TOK), F32),
            jax.ShapeDtypeStruct((3, width, hidden), BF16),
        ),
        in_specs=[vmem] * 4 + [hbm] * 3,
        out_specs=(vmem, vmem, hbm),
        scratch_shapes=[
            *[pltpu.VMEM((width, hidden), BF16)] * 3,
            pltpu.VMEM((TOKENS, TOKENS), BF16),
            *[pltpu.VMEM((NY, PAD, 2 * width + LANES), BF16)] * 2,
            pltpu.VMEM((2, RING, UNIT_TOK, 2 * width + LANES), BF16),
            pltpu.VMEM((CHUNKS, SLOTS, width), BF16),
            pltpu.VMEM((CHUNKS, SLOTS, width), BF16),
            pltpu.VMEM((CHUNKS, SLOTS, LANES), F32),
            pltpu.VMEM((CHUNKS, NY, PART, three), BF16),
            pltpu.VMEM((CHUNKS, 2, PART, three // 2), BF16),
            pltpu.VMEM((CHUNKS, 2, PART, three), BF16),
            pltpu.VMEM((CHUNKS, NY, PART, three), BF16),
            pltpu.VMEM((CHUNKS, SPAN, 2, UNIT, width + LANES), BF16),
            pltpu.VMEM((CHUNKS, SPAN, UNIT, width + LANES), BF16),
            pltpu.VMEM((CHUNKS, SPAN, UNIT, width + LANES), BF16),
            pltpu.VMEM((RING, UNIT, width + LANES), BF16),
            pltpu.VMEM((NY, PAD, width + LANES), BF16),
            pltpu.VMEM((NY, PAD, width + LANES), BF16),
            pltpu.VMEM((width, three), F32),
            pltpu.VMEM((3, width, hidden), BF16),
            pltpu.SemaphoreType.DMA((2, NY)),
            pltpu.SemaphoreType.DMA((2, NZ)),
            pltpu.SemaphoreType.DMA((2, CHUNKS)),
            pltpu.SemaphoreType.DMA((2, CHUNKS)),
            pltpu.SemaphoreType.DMA((2, 2, 2, CHUNKS)),
            pltpu.SemaphoreType.DMA((2, 2, 2, CHUNKS)),
            pltpu.SemaphoreType.DMA((2, CHUNKS)),
            pltpu.SemaphoreType.DMA((RING,)),
            pltpu.SemaphoreType.DMA((RING,)),
            pltpu.SemaphoreType.DMA((2, NY)),
            pltpu.SemaphoreType.DMA((6,)),
        ],
        compiler_params=pltpu.CompilerParams(
            collective_id=0, has_side_effects=True, vmem_limit_bytes=62 * 1024 * 1024
        ),
    )(
        tokens_in[0].transpose(1, 0, 2),
        cotangent[0].transpose(1, 0, 2),
        expert_ids[0].transpose(0, 2, 1),
        gate_probs[0].transpose(0, 2, 1),
        gate_weight[0],
        up_weight[0],
        down_weight[0],
    )
    weights = jax.ShapeDtypeStruct((1, width, hidden), BF16)
    token_grad, route_grad, *grads = pl.pallas_call(
        finish,
        out_shape=(
            jax.ShapeDtypeStruct((1, 1, TOK, NY * width), BF16),
            jax.ShapeDtypeStruct((1, 1, TOP, TOK), BF16),
            weights,
            weights,
            weights,
        ),
        in_specs=[vmem, vmem, hbm],
        out_specs=(vmem, vmem, hbm, hbm, hbm),
        scratch_shapes=[pltpu.VMEM((3, width, hidden), BF16), pltpu.SemaphoreType.DMA((2, 3))],
    )(*out)
    return token_grad, route_grad.transpose(0, 1, 3, 2), *grads


def solution(mesh):
    return jax.shard_map(
        on_device,
        mesh=mesh,
        in_specs=(
            P(("expert", "dp"), None, None, None),
            P(("expert", "dp"), None, None, None),
            P(("expert", "dp"), None, None, None),
            P(("expert", "dp"), None, None, None),
            P("expert", "dp", "half"),
            P("expert", "dp", "half"),
            P("expert", "dp", "half"),
        ),
        out_specs=(
            P(("expert", "dp"), "half", None, None),
            P(("expert", "dp"), "half", None, None),
            P("expert", "dp", "half"),
            P("expert", "dp", "half"),
            P("expert", "dp", "half"),
        ),
        check_vma=False,
    )
```

```python
import functools

import jax
import jax.numpy as jnp
from jax import lax
from jax.experimental import pallas as pl
from jax.experimental.pallas import tpu as pltpu
from jax.sharding import PartitionSpec as P

MESH = pl.DeviceIdType.MESH
BF16 = jnp.bfloat16
F32 = jnp.float32

TOP = 8
MOST = 6
TOK = 12
PAD = 16
NX, NY, NZ = 4, 4, 8
RING = NX * NZ
LAST = NZ // 2
SPAN = 2
CHUNKS = RING // SPAN
UNIT_TOK = NY * TOK
UNIT = NY * MOST
TOKENS = 2 * SPAN * UNIT_TOK
SLOTS = 2 * SPAN * UNIT
PART = SLOTS // NY
LANES = 128


def rem(a, b):
    return lax.rem(a, jnp.int32(b))


def div(a, b):
    return lax.div(a, jnp.int32(b))


def choose(index, values):
    found = jnp.int32(values[0])
    for i, value in enumerate(values[1:], 1):
        if value != values[0]:
            found = jnp.where(index == i, jnp.int32(value), found)
    return found


Z_ORDER = (0, 1, 7, 2, 6, 3, 5, 4)
FIRST_Z = (0, 0, 1, 7, 1, 7, 2, 6, 2, 6, 3, 5, 3, 5, 4, 4)
FIRST_X = (0, 1, 0, 0, 1, 1, 0, 0, 1, 1, 0, 0, 1, 1, 0, 1)
SECOND_X = (0, 0, 0, 0, 1, 3, 1, 3, 1, 3, 1, 3, 2, 2, 2, 2)
SECOND_Z = (0, 1, 2, 3, 0, 0, 1, 1, 2, 2, 3, 3, 0, 1, 2, 3)


def order(n):
    return jnp.where(n < 4, n, jnp.where(n == CHUNKS - 1, 4, n + 1))


def owner(expert, half, c, j):
    x, z = div(expert, NZ), rem(expert, NZ)
    first = rem(x + choose(c, FIRST_X) * SPAN + j, NX) * NZ + rem(z + choose(c, FIRST_Z), NZ)
    z_step = choose(choose(c, SECOND_Z) * SPAN + j, Z_ORDER)
    second = rem(x + choose(c, SECOND_X), NX) * NZ + rem(z + z_step, NZ)
    return first + half * (second - first)


def index_of(shape, dim):
    return lax.broadcasted_iota(jnp.int32, shape, dim).astype(F32)


def whole(number, size):
    return jnp.floor((number + 0.5) * (1.0 / size))


def part_of(number, size):
    return number - size * whole(number, size)


def before(size, span):
    row, col = index_of((size, size), 0), index_of((size, size), 1)
    return jnp.where((whole(row, span) == whole(col, span)) & (row < col), 1.0, 0.0).astype(BF16)


def matmul(a, b, a_dim=1, b_dim=0):
    return lax.dot_general(a, b, (((a_dim,), (b_dim,)), ((), ())), preferred_element_type=F32)


def kernel(
    width,
    hidden,
    tokens,
    cotangent,
    ids,
    probs,
    w_gate_hbm,
    w_up_hbm,
    w_down_hbm,
    token_out,
    route_out,
    grads_hbm,
    w_gate,
    w_up,
    w_down,
    before_chunk,
    stage,
    own,
    units,
    slot_x,
    slot_s,
    gates,
    part,
    sum_one,
    sum_two,
    act,
    row_part,
    row_other,
    row_send,
    row_back,
    fin_send,
    fin_recv,
    acc,
    grads_out,
    own_sem,
    near_sem,
    far_sem,
    twin_sem,
    sum_sem,
    act_sem,
    half_sem,
    back_send,
    back_recv,
    fin_sem,
    load_sem,
):
    loads = [
        pltpu.make_async_copy(src, dst, load_sem.at[n])
        for n, (src, dst) in enumerate(((w_gate_hbm, w_gate), (w_up_hbm, w_up), (w_down_hbm, w_down)))
    ]
    for load in loads:
        load.start()
    expert, half, dp = lax.axis_index("expert"), lax.axis_index("half"), lax.axis_index("dp")
    other = 1 - half
    x, z = div(expert, NZ), rem(expert, NZ)
    z_next, z_last = x * NZ + rem(z + 1, NZ), x * NZ + rem(z + NZ - 1, NZ)
    z_two_next, z_two_last = x * NZ + rem(z + 2, NZ), x * NZ + rem(z + NZ - 2, NZ)
    x_at = [rem(x + r, NX) * NZ + z for r in range(NX)]
    y_next, y_last, y_far = rem(dp + 1, NY), rem(dp + 3, NY), rem(dp + 2, NY)
    three = 3 * hidden
    mid = three // 2

    def remote(src, dst, send, recv, where):
        return pltpu.make_async_remote_copy(
            src_ref=src, dst_ref=dst, send_sem=send, recv_sem=recv, device_id=where, device_id_type=MESH
        )

    barrier = pltpu.get_barrier_semaphore()

    def greet(i, carry):
        pl.semaphore_signal(
            barrier, inc=1, device_id={"expert": rem(expert + i, RING)}, device_id_type=MESH
        )
        return carry

    lax.fori_loop(1, RING, greet, 0)
    for r in range(1, NY):
        pl.semaphore_signal(barrier, inc=1, device_id={"dp": rem(dp + r, NY)}, device_id_type=MESH)
    pl.semaphore_signal(barrier, inc=1, device_id={"half": other}, device_id_type=MESH)
    acc[...] = jnp.zeros_like(acc)
    before_chunk[...] = before(TOKENS, TOK)
    row, col = index_of((PAD, 2 * TOK), 0), index_of((PAD, 2 * TOK), 1)
    mine = jnp.where((row < TOK) & (col == 2 * row + half), 1.0, 0.0).astype(BF16)
    block_x = matmul(mine, tokens[...].reshape(2 * TOK, NY * width)).astype(BF16)
    block_d = matmul(mine, cotangent[...].reshape(2 * TOK, NY * width)).astype(BF16)
    named, weight = ids[half], probs[half].astype(F32)
    lane = lax.broadcasted_iota(jnp.int32, (LANES, TOK), 0)
    gate_map = jnp.zeros((LANES, TOK), F32)
    for k in range(TOP):
        gate_map = jnp.where(named[k : k + 1] == lane, weight[k : k + 1], gate_map)
    unit = jnp.where(index_of((PAD, TOK), 0) == index_of((PAD, TOK), 1), 1.0, 0.0).astype(BF16)
    gate_map = matmul(unit, gate_map.astype(BF16), 1, 1).astype(BF16)
    for q in range(NY):
        stage[q, :, 0:width] = block_x[:, q * width : (q + 1) * width]
        stage[q, :, width : width + LANES] = gate_map
        stage[q, :, width + LANES :] = block_d[:, q * width : (q + 1) * width]
    own[dp] = stage[dp]
    row, col = index_of((UNIT_TOK, NY * PAD), 0), index_of((UNIT_TOK, NY * PAD), 1)
    same = (whole(row, TOK) == whole(col, PAD)) & (part_of(row, TOK) == part_of(col, PAD))
    squeeze = jnp.where(same, 1.0, 0.0).astype(BF16)
    pl.semaphore_wait(barrier, RING - 1 + NY - 1 + 1)

    def own_copy(r):
        return remote(
            stage.at[rem(dp + r, NY)],
            own.at[dp],
            own_sem.at[0, r],
            own_sem.at[1, r],
            {"dp": rem(dp + r, NY)},
        )

    def own_arrival(r):
        source = rem(dp + NY - r, NY)
        return remote(stage.at[source], own.at[source], own_sem.at[0, r], own_sem.at[1, r], {"dp": source})

    for r in range(1, NY):
        own_copy(r).start()
    for r in range(1, NY):
        own_arrival(r).wait_recv()
    own_rows = own[...].reshape(NY * PAD, 2 * width + LANES)
    packed = matmul(squeeze, own_rows).astype(BF16)
    units[half, 0] = packed

    def near(src, dst, toward):
        return remote(
            units.at[half, src],
            units.at[half, dst],
            near_sem.at[0, dst],
            near_sem.at[1, dst],
            {"expert": toward},
        )

    def far(src, dst, toward):
        return remote(
            units.at[half, pl.ds(src * SPAN, SPAN)],
            units.at[half, pl.ds(dst * SPAN, SPAN)],
            far_sem.at[0, dst],
            far_sem.at[1, dst],
            {"expert": toward},
        )

    def near_wait(dst):
        near(dst, dst, z_next).wait_recv()

    def near_pass(src, dst, toward):
        near(src, dst, toward).start()

    def far_wait(dst):
        far(dst, dst, z_next).wait_recv()

    def far_pass(src, dst, toward):
        far(src, dst, toward).start()

    @pl.when(half == 0)
    def _():
        near_pass(0, 1, x_at[3])
        near_pass(0, 3, x_at[1])

    @pl.when(half == 1)
    def _():
        near_pass(0, 1, z_last)
        near_pass(0, 2, z_next)

    def take_first(c):
        @pl.when(c == 0)
        def _():
            near_wait(1)
            near_pass(0, 2, x_at[2])

        @pl.when(c == 1)
        def _():
            near_wait(3)
            near_wait(2)

        @pl.when(c > 1)
        def _():
            far_wait(c)

        @pl.when(c < 2)
        def _():
            far_pass(c, 2 * c + 2, z_last)
            far_pass(c, 2 * c + 3, z_next)

        even = rem(c, 2) == 0

        @pl.when((c > 1) & (c < 11) & even)
        def _():
            far_pass(c, c + 4, z_last)

        @pl.when((c > 1) & (c < 10) & jnp.logical_not(even))
        def _():
            far_pass(c, c + 4, z_next)

        @pl.when(c == 13)
        def _():
            far_pass(c, 15, z_next)

    def take_second(c):
        @pl.when(c == 0)
        def _():
            near_wait(1)
            near_pass(0, 3, z_two_last)
            near_pass(0, 4, z_two_next)

        @pl.when(c == 1)
        def _():
            near_wait(2)
            near_wait(3)
            near_pass(3, 5, z_last)

        @pl.when(c == 2)
        def _():
            near_wait(4)
            near_pass(4, 6, z_next)
            near_wait(5)
            near_pass(5, 7, z_last)

        @pl.when(c == 3)
        def _():
            near_wait(6)
            near_wait(7)

        @pl.when(c > 3)
        def _():
            far_wait(c)

        @pl.when(c < 4)
        def _():
            far_pass(c, 2 * c + 4, x_at[3])
            far_pass(c, 2 * c + 5, x_at[1])

        @pl.when((c == 4) | (c == 6))
        def _():
            far_pass(c, 10 + div(c, 2), x_at[3])

        @pl.when((c == 9) | (c == 11))
        def _():
            far_pass(c, 10 + div(c, 2), x_at[1])

    def take(c):
        pl.when(half == 0)(functools.partial(take_first, c))
        pl.when(half == 1)(functools.partial(take_second, c))
        twin(c, half).start()

    def twin(c, block):
        span = pl.ds(c * SPAN, SPAN)
        return remote(
            units.at[block, span],
            units.at[block, span],
            twin_sem.at[0, c],
            twin_sem.at[1, c],
            {"half": other},
        )

    def sum_copy(stage_no, c, way, src, dst):
        return remote(
            src,
            dst,
            sum_sem.at[stage_no, 0, way, c],
            sum_sem.at[stage_no, 1, way, c],
            {"dp": y_next if way == 0 else y_last},
        )

    def act_copy(stage_no, c, way, view):
        return remote(
            view,
            view,
            act_sem.at[stage_no, 0, way, c],
            act_sem.at[stage_no, 1, way, c],
            {"dp": y_next if way == 0 else y_last},
        )

    def columns(way):
        return pl.ds(way * mid, mid)

    def first_sum(c, way):
        return sum_copy(0, c, way, part.at[c, y_far, :, columns(way)], sum_one.at[c, way])

    def second_sum(c, way):
        toward = y_next if way == 0 else y_last
        return sum_copy(1, c, way, part.at[c, toward], sum_two.at[c, way])

    def select(c):
        chunk = order(c)
        twin(chunk, other).wait_recv()
        span = pl.ds(chunk * SPAN, SPAN)
        stacked = jnp.concatenate(
            [units[b, span].reshape(SPAN * UNIT_TOK, 2 * width + LANES) for b in range(2)], axis=0
        )
        is_expert = lax.broadcasted_iota(jnp.int32, (8, LANES), 1) == expert
        gate_row = matmul(is_expert.astype(BF16), stacked[:, width : width + LANES], 1, 1)
        chosen = gate_row > 0.0
        rank = matmul(chosen.astype(BF16), before_chunk[...])
        token = index_of((8, TOKENS), 1)
        unit = whole(token, UNIT_TOK)
        unit = part_of(unit, SPAN) * 2 + whole(unit, SPAN)
        base = unit * UNIT + part_of(whole(token, TOK), NY) * MOST
        place = jnp.where(chosen, base + rank, -1.0)
        pick = jnp.where(index_of((SLOTS, TOKENS), 0) == place[:1], 1.0, 0.0).astype(BF16)
        gate_wide = matmul(
            pick, jnp.broadcast_to(gate_row[:1], (LANES, TOKENS)).astype(BF16), 1, 1
        )
        gates[c] = gate_wide
        slots = matmul(pick, stacked[:, :width]).astype(BF16)
        slot_x[c] = slots
        slots_d = matmul(pick, stacked[:, width + LANES :])
        slot_s[c] = (gate_wide[:, :1] * slots_d).astype(BF16)
        shape = (NY, PART, hidden)
        part[c, :, :, 0:hidden] = matmul(slots, w_gate[...]).astype(BF16).reshape(shape)
        part[c, :, :, hidden : 2 * hidden] = matmul(slots, w_up[...]).astype(BF16).reshape(shape)
        part[c, :, :, 2 * hidden :] = (
            matmul(slots_d.astype(BF16), w_down[...]).astype(BF16).reshape(shape)
        )
        for way in range(2):
            first_sum(c, way).start()

    def add_passing(c):
        for way in range(2):
            first_sum(c, way).wait_recv()
            toward = y_next if way == 0 else y_last
            here = part[c, toward, :, columns(way)].astype(F32)
            part[c, toward, :, columns(way)] = (here + sum_one[c, way].astype(F32)).astype(BF16)
            second_sum(c, way).start()

    def activate(c):
        for way in range(2):
            second_sum(c, way).wait_recv()
        summed = (
            part[c, dp].astype(F32) + sum_two[c, 0].astype(F32) + sum_two[c, 1].astype(F32)
        )
        gate_act, up_act, back = (
            summed[:, :hidden],
            summed[:, hidden : 2 * hidden],
            summed[:, 2 * hidden :],
        )
        gate_col = gates[c, pl.ds(pl.multiple_of(dp * PART, PART), PART), :][:, :1]
        sigma = jax.nn.sigmoid(gate_act)
        active = gate_act * sigma
        slope = sigma * (1.0 + gate_act * (1.0 - sigma))
        units = (active * up_act).astype(BF16)
        scaled_back = gate_col * back
        act[c, dp, :, 0:hidden] = (scaled_back * up_act * slope).astype(BF16)
        act[c, dp, :, hidden : 2 * hidden] = (scaled_back * active).astype(BF16)
        act[c, dp, :, 2 * hidden :] = units
        route = jnp.sum(back * units.astype(F32), axis=1, keepdims=True)
        gates[c] = jnp.zeros((SLOTS, LANES), F32)
        gates[c, pl.ds(pl.multiple_of(dp * PART, PART), PART), :] = jnp.broadcast_to(
            route, (PART, LANES)
        )
        for way in range(2):
            act_copy(0, c, way, act.at[c, dp]).start()

    def pass_act(c):
        for way in range(2):
            source = y_last if way == 0 else y_next
            act_copy(0, c, way, act.at[c, source]).wait_recv()
            act_copy(1, c, way, act.at[c, source, :, columns(way)]).start()

    def half_copy(c):
        return remote(
            row_part.at[c, :, other],
            row_other.at[c],
            half_sem.at[0, c],
            half_sem.at[1, c],
            {"half": other},
        )

    def row_terms(c):
        for way in range(2):
            act_copy(1, c, way, act.at[c, y_far, :, columns(way)]).wait_recv()
        grads = act[c].reshape(SLOTS, three)
        rows = matmul(grads[:, :hidden], w_gate[...], 1, 1) + matmul(
            grads[:, hidden : 2 * hidden], w_up[...], 1, 1
        )
        row_part[c, :, :, :, 0:width] = rows.astype(BF16).reshape(SPAN, 2, UNIT, width)
        row_part[c, :, :, :, width:] = gates[c].astype(BF16).reshape(SPAN, 2, UNIT, LANES)
        half_copy(c).start()

    def back_copy(place, c, j, toward):
        return remote(
            row_send.at[c, j],
            row_back.at[expert],
            back_send.at[place],
            back_recv.at[expert],
            {"expert": toward},
        )

    def give_back(c):
        half_copy(c).wait_recv()
        for j in range(SPAN):
            place = c * SPAN + j
            row_send[c, j] = (
                row_part[c, j, half].astype(F32) + row_other[c, j].astype(F32)
            ).astype(BF16)
            toward = owner(expert, half, order(c), j)

            @pl.when(place != 0)
            def _():
                back_copy(place, c, j, toward).start()

            @pl.when(place == 0)
            def _():
                row_back[expert] = row_send[c, j]

    def weight_terms(c):
        pair = pl.ds(c - 1, 2)

        def tile(m, carry):
            span = pl.ds(pl.multiple_of(m * LANES, LANES), LANES)
            acc[span, : 2 * hidden] += matmul(
                slot_x[pair, :, span].reshape(2 * SLOTS, LANES),
                act[pair, :, :, : 2 * hidden].reshape(2 * SLOTS, 2 * hidden),
                0,
                0,
            )
            acc[span, 2 * hidden :] += matmul(
                slot_s[pair, :, span].reshape(2 * SLOTS, LANES),
                act[pair, :, :, 2 * hidden :].reshape(2 * SLOTS, hidden),
                0,
                0,
            )
            return carry

        @pl.when(rem(c, 2) == 1)
        def _():
            lax.fori_loop(0, width // LANES, tile, 0)

    for load in loads:
        load.wait()

    def sent(c):
        twin(c, half).wait_send()
        for way in range(2):
            first_sum(c, way).wait_send()
            second_sum(c, way).wait_send()
            act_copy(0, c, way, act.at[c, dp]).wait_send()
            act_copy(1, c, way, act.at[c, y_far, :, columns(way)]).wait_send()
        half_copy(c).wait_send()

        @pl.when(c == 0)
        def _():
            for dst in range(1, NX):
                near(0, dst, z_next).wait_send()

        @pl.when((c == 0) & (half == 1))
        def _():
            for dst in range(NX, NZ):
                near(0, dst, z_next).wait_send()

        @pl.when((c > 3) | ((c > 1) & (half == 0)))
        def _():
            far(0, c, z_next).wait_send()

        @pl.when(c == 2)
        def _():
            back_copy(1, 0, 0, z_next).wait_send()

        @pl.when(c > 2)
        def _():
            for j in range(SPAN):
                back_copy((c - 2) * SPAN + j, 0, 0, z_next).wait_send()

    def turn(i, carry):
        def staged(lag, work):
            pl.when((i >= lag) & (i - lag < CHUNKS))(functools.partial(work, i - lag))

        staged(6, pass_act)
        staged(3, add_passing)
        staged(7, row_terms)
        staged(1, select)
        staged(4, activate)
        first = i + jnp.where(i > 4, 1, 0)
        beyond = jnp.minimum(i + 1 + jnp.where(i > 3, 1, 0), CHUNKS)

        def take_one(c, carry):
            take(c)
            return carry

        lax.fori_loop(first, beyond, take_one, 0)
        staged(7, give_back)
        staged(8, weight_terms)
        staged(9, sent)
        return carry

    lax.fori_loop(0, CHUNKS + 9, turn, 0)

    stores = []
    for n in range(3):
        grads_out[n] = acc[:, n * hidden : (n + 1) * hidden].astype(BF16)
        stores.append(pltpu.make_async_copy(grads_out.at[n], grads_hbm.at[n], load_sem.at[3 + n]))
        stores[n].start()

    own_gate = own_rows[:, width : width + LANES]
    own_chosen = (own_gate.astype(F32) > 0.0).astype(BF16)
    own_rank = matmul(before(NY * PAD, PAD), own_chosen, 0, 0).astype(BF16)
    returns = RING * UNIT
    spread = jnp.where(
        index_of((LANES, returns), 0) == whole(index_of((LANES, returns), 1), UNIT), 1.0, 0.0
    ).astype(BF16)
    chosen_at = matmul(own_chosen, spread)
    rank_at = matmul(own_rank, spread)
    own_token, slot = index_of((NY * PAD, returns), 0), index_of((NY * PAD, returns), 1)
    fits = (rank_at == part_of(slot, MOST)) & (
        whole(own_token, PAD) == part_of(whole(slot, MOST), NY)
    )
    combine = jnp.where(fits, chosen_at, 0.0).astype(BF16)
    gather = jnp.where(
        whole(index_of((returns, LANES), 0), UNIT) == index_of((returns, LANES), 1), 1.0, 0.0
    ).astype(BF16)

    def arrival(i, carry):
        source = rem(expert + i, RING)
        remote(
            row_send.at[0, 0],
            row_back.at[source],
            back_send.at[0],
            back_recv.at[source],
            {"expert": source},
        ).wait_recv()
        return carry

    lax.fori_loop(1, RING, arrival, 0)
    returned = row_back[...].reshape(RING * UNIT, width + LANES)
    token_sum = matmul(combine, returned[:, :width])
    route_sum = matmul(combine, returned[:, width:] * gather)
    fin_send[:, :, 0:width] = token_sum.astype(BF16).reshape(NY, PAD, width)
    fin_send[:, :, width:] = route_sum.astype(BF16).reshape(NY, PAD, LANES)

    def fin_copy(r):
        return remote(
            fin_send.at[rem(dp + r, NY)],
            fin_recv.at[dp],
            fin_sem.at[0, r],
            fin_sem.at[1, r],
            {"dp": rem(dp + r, NY)},
        )

    def fin_arrival(r):
        source = rem(dp + NY - r, NY)
        return remote(
            fin_send.at[source], fin_recv.at[source], fin_sem.at[0, r], fin_sem.at[1, r], {"dp": source}
        )

    for r in range(1, NY):
        fin_copy(r).start()
    fin_recv[dp] = fin_send[dp]
    for r in range(1, NY):
        fin_arrival(r).wait_recv()
    routes = jnp.zeros((PAD, LANES), F32)
    for q in range(NY):
        token_out[:, q * width : (q + 1) * width] = fin_recv[q, :, 0:width]
        routes = routes + fin_recv[q, :, width:].astype(F32)
    unit = jnp.where(index_of((LANES, LANES), 0) == index_of((LANES, LANES), 1), 1.0, 0.0)
    by_expert = matmul(unit.astype(BF16), routes.astype(BF16), 1, 1)[:, :TOK]
    lane = lax.broadcasted_iota(jnp.int32, (LANES, TOK), 0)
    named = ids[half]
    for k in range(TOP):
        value = jnp.where(named[k : k + 1] == lane, by_expert, 0.0)
        route_out[k : k + 1] = jnp.sum(value, axis=0, keepdims=True)
    for store in stores:
        store.wait()
    for r in range(1, NY):
        own_copy(r).wait_send()
        fin_copy(r).wait_send()

    for place in range((CHUNKS - 2) * SPAN, RING):
        back_copy(place, 0, 0, z_next).wait_send()


def finish(token_rows, route_rows, grads, token_out, route_out, gate_out, up_out, down_out, held, sem):
    targets = (gate_out, up_out, down_out)
    loads = [pltpu.make_async_copy(grads.at[n], held.at[n], sem.at[0, n]) for n in range(3)]
    stores = [pltpu.make_async_copy(held.at[n], targets[n].at[0], sem.at[1, n]) for n in range(3)]
    for load in loads:
        load.start()
    token_out[0, 0] = token_rows[:TOK]
    route_out[0, 0] = route_rows[...].astype(BF16)
    for load, store in zip(loads, stores):
        load.wait()
        store.start()
    for store in stores:
        store.wait()


def on_device(tokens_in, cotangent, expert_ids, gate_probs, gate_weight, up_weight, down_weight):
    width, hidden = gate_weight.shape[1], gate_weight.shape[2]
    three = 3 * hidden
    vmem = pl.BlockSpec(memory_space=pltpu.VMEM)
    hbm = pl.BlockSpec(memory_space=pl.ANY)
    out = pl.pallas_call(
        functools.partial(kernel, width, hidden),
        out_shape=(
            jax.ShapeDtypeStruct((PAD, NY * width), BF16),
            jax.ShapeDtypeStruct((TOP, TOK), F32),
            jax.ShapeDtypeStruct((3, width, hidden), BF16),
        ),
        in_specs=[vmem] * 4 + [hbm] * 3,
        out_specs=(vmem, vmem, hbm),
        scratch_shapes=[
            *[pltpu.VMEM((width, hidden), BF16)] * 3,
            pltpu.VMEM((TOKENS, TOKENS), BF16),
            *[pltpu.VMEM((NY, PAD, 2 * width + LANES), BF16)] * 2,
            pltpu.VMEM((2, RING, UNIT_TOK, 2 * width + LANES), BF16),
            pltpu.VMEM((CHUNKS, SLOTS, width), BF16),
            pltpu.VMEM((CHUNKS, SLOTS, width), BF16),
            pltpu.VMEM((CHUNKS, SLOTS, LANES), F32),
            pltpu.VMEM((CHUNKS, NY, PART, three), BF16),
            pltpu.VMEM((CHUNKS, 2, PART, three // 2), BF16),
            pltpu.VMEM((CHUNKS, 2, PART, three), BF16),
            pltpu.VMEM((CHUNKS, NY, PART, three), BF16),
            pltpu.VMEM((CHUNKS, SPAN, 2, UNIT, width + LANES), BF16),
            pltpu.VMEM((CHUNKS, SPAN, UNIT, width + LANES), BF16),
            pltpu.VMEM((CHUNKS, SPAN, UNIT, width + LANES), BF16),
            pltpu.VMEM((RING, UNIT, width + LANES), BF16),
            pltpu.VMEM((NY, PAD, width + LANES), BF16),
            pltpu.VMEM((NY, PAD, width + LANES), BF16),
            pltpu.VMEM((width, three), F32),
            pltpu.VMEM((3, width, hidden), BF16),
            pltpu.SemaphoreType.DMA((2, NY)),
            pltpu.SemaphoreType.DMA((2, NZ)),
            pltpu.SemaphoreType.DMA((2, CHUNKS)),
            pltpu.SemaphoreType.DMA((2, CHUNKS)),
            pltpu.SemaphoreType.DMA((2, 2, 2, CHUNKS)),
            pltpu.SemaphoreType.DMA((2, 2, 2, CHUNKS)),
            pltpu.SemaphoreType.DMA((2, CHUNKS)),
            pltpu.SemaphoreType.DMA((RING,)),
            pltpu.SemaphoreType.DMA((RING,)),
            pltpu.SemaphoreType.DMA((2, NY)),
            pltpu.SemaphoreType.DMA((6,)),
        ],
        compiler_params=pltpu.CompilerParams(
            collective_id=0, has_side_effects=True, vmem_limit_bytes=62 * 1024 * 1024
        ),
    )(
        tokens_in[0].transpose(1, 0, 2),
        cotangent[0].transpose(1, 0, 2),
        expert_ids[0].transpose(0, 2, 1),
        gate_probs[0].transpose(0, 2, 1),
        gate_weight[0],
        up_weight[0],
        down_weight[0],
    )
    weights = jax.ShapeDtypeStruct((1, width, hidden), BF16)
    token_grad, route_grad, *grads = pl.pallas_call(
        finish,
        out_shape=(
            jax.ShapeDtypeStruct((1, 1, TOK, NY * width), BF16),
            jax.ShapeDtypeStruct((1, 1, TOP, TOK), BF16),
            weights,
            weights,
            weights,
        ),
        in_specs=[vmem, vmem, hbm],
        out_specs=(vmem, vmem, hbm, hbm, hbm),
        scratch_shapes=[pltpu.VMEM((3, width, hidden), BF16), pltpu.SemaphoreType.DMA((2, 3))],
    )(*out)
    return token_grad, route_grad.transpose(0, 1, 3, 2), *grads


def solution(mesh):
    return jax.shard_map(
        on_device,
        mesh=mesh,
        in_specs=(
            P(("expert", "dp"), None, None, None),
            P(("expert", "dp"), None, None, None),
            P(("expert", "dp"), None, None, None),
            P(("expert", "dp"), None, None, None),
            P("expert", "dp", "half"),
            P("expert", "dp", "half"),
            P("expert", "dp", "half"),
        ),
        out_specs=(
            P(("expert", "dp"), "half", None, None),
            P(("expert", "dp"), "half", None, None),
            P("expert", "dp", "half"),
            P("expert", "dp", "half"),
            P("expert", "dp", "half"),
        ),
        check_vma=False,
    )
```
